256 devices in a mesh: replica: 16 (over x, z_hi, core), fsdp: 16 (over y, z_lo).
Axes of the slice: x: 4, y: 4, z: 8 (z_hi: 2, z_lo: 4; z = z_hi * 4 + z_lo), core: 2. Of those that a mesh axis runs over, the one named last changes fastest.
Arguments:
- local_weights: float32 [16, 384, 28672], P('replica', None, 'fsdp'), may hold values from -6 to 6
- base_weights: float32 [384, 28672], P(None, 'fsdp'), may hold values from -6 to 6
- error_buffer: float32 [16, 384, 28672], P('replica', None, 'fsdp'), may hold values from -3 to 3
- momentum: float32 [384, 28672], P(None, 'fsdp'), may hold values from -3 to 3
- keep_index: int32 [224, 3, 256], P('fsdp'), may hold values from 0 to 3999, as said below
Outputs:
- new_momentum: float32 [384, 28672], P(None, 'fsdp')
- new_error: float32 [16, 384, 28672], P('replica', None, 'fsdp')
- weights: bfloat16 [384, 28672], replicated
The draws below stay inside these ranges and needn't reach their ends.
Inputs may be any that keep to these rules, and one draw needn't show every extreme that they name: keep_index[j, i] lists 256 distinct positions u * 128 + v with u and v below 32; every block lists position 0 and the position with u = v = 31; the same positions serve all replicas.
All inputs are finite; a program needn't handle non-finite values.
Results may differ from the reference program's by a relative error of at most 0.0065.
Values may be sent and summed in bfloat16 or wider, within the bound.
A program may use at most 192 MiB of HBM per device.

```python
import jax
import jax.numpy as jnp
from jax import lax

FF = 28672
ROWS = 384
BLOCK = 128
LOWF = 32
KEEP = 256
N_REPLICA = 16


def draw_keep_index(key, part):
    key = jax.random.fold_in(key, 7)
    block_total = FF // BLOCK * (ROWS // BLOCK)
    block_keys = jax.random.split(key, block_total)
    chosen = jax.vmap(lambda subkey: jax.random.permutation(subkey, LOWF * LOWF - 2)[:KEEP - 2] + 1)(block_keys)
    zeros_column = jnp.zeros((block_total, 1), jnp.int32)
    corner_column = jnp.full((block_total, 1), LOWF * LOWF - 1, jnp.int32)
    lattice = jnp.concatenate([zeros_column, chosen.astype(jnp.int32), corner_column], axis=1)
    position = lattice // LOWF * BLOCK + lattice % LOWF
    return position.reshape(FF // BLOCK, ROWS // BLOCK, KEEP).astype(jnp.int32)


def shard_levels(rng, extent, pieces, smallest, top_value):
    factor_of = 1.0
    for dim, parts in pieces:
        steps = jax.random.uniform(jax.random.fold_in(jax.random.fold_in(rng, 6), dim), (parts,), jnp.float32, smallest / len(pieces), top_value / len(pieces))
        factor_of = factor_of * jnp.repeat(jnp.exp(steps), extent[dim] // parts).reshape((-1,) + (1,) * (len(extent) - 1 - dim))
    return factor_of


def normal_values(rng, shape, deviation, limit, shards=(), kind=jnp.bfloat16):
    entries = jax.random.normal(rng, shape, jnp.float32) * deviation
    if len(shards) > 0:
        entries = shard_levels(rng, shape, shards, -0.22, 0.18) * entries
    return jnp.clip(entries, min=-limit, max=limit).astype(kind)


def setup_inputs(seed: int = 0) -> dict:
    splits = jax.random.split(jax.random.key(seed), 6)
    local_weights = normal_values(splits[0], (N_REPLICA, ROWS, FF), 1.0, 6.0, ((0, 16), (2, 16)), jnp.float32)
    base_weights = normal_values(splits[1], (ROWS, FF), 1.0, 6.0, ((1, 16),), jnp.float32)
    error_buffer = normal_values(splits[2], (N_REPLICA, ROWS, FF), 0.5, 3.0, ((0, 16), (2, 16)), jnp.float32)
    momentum = normal_values(splits[3], (ROWS, FF), 0.5, 3.0, ((1, 16),), jnp.float32)
    keep_index = draw_keep_index(jax.random.fold_in(splits[5], 71), 0)
    return {"local_weights": local_weights, "base_weights": base_weights, "error_buffer": error_buffer, "momentum": momentum, "keep_index": keep_index}


outer_rate = 0.7
outer_momentum = 0.9

def dct_table(length):
    frequency = jnp.arange(length, dtype=jnp.float32)[:, None]
    position = jnp.arange(length, dtype=jnp.float32)[None, :]
    norm_scale = jnp.where(frequency == 0, jnp.sqrt(1.0 / length), jnp.sqrt(2.0 / length))
    return norm_scale * jnp.cos(jnp.pi * (2.0 * position + 1.0) * frequency / (2.0 * length))

def encode(blocks, cosine_table):
    halfway = jnp.einsum('iajb,vb->iajv', blocks, cosine_table, precision=lax.Precision.HIGHEST)
    return jnp.einsum('ua,iajv->iujv', cosine_table, halfway, precision=lax.Precision.HIGHEST)

def decode(blocks, cosine_table):
    halfway = jnp.einsum('iujv,vb->iujb', blocks, cosine_table, precision=lax.Precision.HIGHEST)
    return jnp.einsum('ua,iujb->iajb', cosine_table, halfway, precision=lax.Precision.HIGHEST)

def pack_blocks(coefficients, positions):
    col_blocks, row_blocks, slots = positions.shape
    flat = coefficients.transpose(2, 0, 1, 3).reshape(col_blocks, row_blocks, BLOCK * BLOCK)
    return jnp.take_along_axis(flat, positions, axis=2)

def unpack_blocks(packed, positions):
    col_blocks, row_blocks, slots = positions.shape
    flat = jnp.zeros((col_blocks, row_blocks, BLOCK * BLOCK), packed.dtype)
    column_index = jnp.arange(col_blocks, dtype=jnp.int32)[:, None, None]
    row_index = jnp.arange(row_blocks, dtype=jnp.int32)[None, :, None]
    flat = flat.at[column_index, row_index, positions].set(packed)
    return flat.reshape(col_blocks, row_blocks, BLOCK, BLOCK).transpose(1, 2, 0, 3)

def reference(local_weights, base_weights, error_buffer, momentum, keep_index):
    cosine_table = dct_table(BLOCK)
    row_blocks = ROWS // BLOCK
    col_blocks = FF // BLOCK

    def one_replica(pair):
        local_slab, error_slab = pair
        pseudo_gradient = base_weights - local_slab + error_slab
        coefficients = encode(pseudo_gradient.reshape(row_blocks, BLOCK, col_blocks, BLOCK), cosine_table)
        packed = pack_blocks(coefficients, keep_index)
        kept_blocks = unpack_blocks(packed, keep_index)
        fresh_error = pseudo_gradient - decode(kept_blocks, cosine_table).reshape(ROWS, FF)
        return (packed, fresh_error)
    packed_all, new_error = lax.map(one_replica, (local_weights, error_buffer))
    mean_coefficients = lax.optimization_barrier(jnp.sum(packed_all, axis=0)) / N_REPLICA
    update = decode(unpack_blocks(mean_coefficients, keep_index), cosine_table).reshape(ROWS, FF)
    new_momentum = outer_momentum * momentum + update
    weights = (base_weights - outer_rate * (update + outer_momentum * new_momentum)).astype(jnp.bfloat16)
    return (new_momentum, new_error, weights)
```

```python
import functools

import jax
import jax.numpy as jnp
import ml_dtypes
import numpy as np
from jax import lax
from jax.experimental import pallas as pl
from jax.experimental.pallas import tpu as pltpu
from jax.sharding import PartitionSpec as P

MESH = pl.DeviceIdType.MESH
BLOCK = 128
LOWF = 32
N_REPLICA = 16
F32 = jnp.float32
BF16 = jnp.bfloat16
outer_rate = 0.7
outer_momentum = 0.9

TILES = ((0, 512), (512, 512), (1024, 512), (1536, 256))
STAGES = ((0, 96, 32, 32), (192, 96, 32, 32))


def split(values):
    high = values.astype(ml_dtypes.bfloat16)
    low = (values - high.astype(np.float64)).astype(ml_dtypes.bfloat16)
    return high, low


def tables():
    u = np.arange(LOWF, dtype=np.float64)[:, None]
    a = np.arange(BLOCK, dtype=np.float64)[None, :]
    norm = np.where(u == 0, np.sqrt(1.0 / BLOCK), np.sqrt(2.0 / BLOCK))
    low = norm * np.cos(np.pi * (2 * a + 1) * u / (2 * BLOCK))
    diag = np.kron(np.eye(4), low)
    wide = np.concatenate(split(diag), axis=0)
    turned = np.zeros((BLOCK, BLOCK))
    turned[:, :LOWF] = low.T
    narrow = np.concatenate(split(diag.T) + split(low) + split(turned), axis=0)
    return wide, narrow


def mm(a, b):
    return jnp.dot(a, b, preferred_element_type=F32)


def halves(v):
    high = v.astype(BF16)
    return high, (v - high.astype(F32)).astype(BF16)


def three(a, b):
    return mm(a[0], b[0]) + (mm(a[1], b[0]) + mm(a[0], b[1]))


def kernel(
    local_hbm, base_hbm, err_hbm, mom_hbm, keep_hbm, wide_hbm, narrow_hbm,
    z_ref, e_ref, m_ref,
    local, base, err, mom, keep, wide, narrow,
    mask, kept, rs_send, rs_recv, part, mean,
    load_sem, red_send, red_recv, out_sem, in_sem, pair_sem,
):
    r, f = lax.axis_index("replica"), lax.axis_index("fsdp")
    x, zh, c = r // 4, (r // 2) % 2, r % 2
    y, zl = f // 4, f % 4
    z = zh * 4 + zl
    cols = e_ref.shape[1]
    group = x * 2 + c

    def at(x_, y_, z_, c_):
        return ((x_ * 2 + z_ // 4) * 2 + c_, y_ * 4 + z_ % 4)

    device = {
        "x+": at((x + 1) % 4, y, z, c), "x-": at((x + 3) % 4, y, z, c),
        "y+": at(x, (y + 1) % 4, z, c), "y-": at(x, (y + 3) % 4, z, c),
        "z+": at(x, y, (z + 1) % 8, c), "z-": at(x, y, (z + 7) % 8, c),
        "far": at(x, y, (z + 4) % 8, c), "pair": at(x, y, z, 1 - c),
    }
    peers = [(group + k) % 8 for k in range(1, 8)]
    peer_device = [at(p // 2, y, z, p % 2) for p in peers]

    def load(src, dst, n):
        copy = pltpu.make_async_copy(src, dst, load_sem.at[n])
        copy.start()
        return copy

    loads = {"keep": load(keep_hbm, keep, 0), "narrow": load(narrow_hbm, narrow, 1)}
    for i in range(3):
        rows = pl.ds(BLOCK * i, BLOCK)
        loads["base", i] = load(base_hbm.at[rows], base.at[rows], 2 + i)
        loads["local", i] = load(local_hbm.at[0, rows], local.at[rows], 5 + i)
        loads["err", i] = load(err_hbm.at[0, rows], err.at[rows], 8 + i)
    loads["wide"] = load(wide_hbm, wide, 11)
    loads["mom"] = load(mom_hbm, mom, 12)

    barrier = pltpu.get_barrier_semaphore()
    partners = [device[k] for k in ("y+", "y-", "z+", "z-", "far")] + peer_device
    for d in partners:
        pl.semaphore_signal(barrier, inc=1, device_id=d, device_id_type=MESH)

    loads["keep"].wait()
    for i in range(3):
        for t, (_, width) in enumerate(TILES):
            n = width // BLOCK
            at_u, at_v = [], []
            for b in range(n):
                pos = keep[i, pl.ds(4 * t + b, 1), :]
                u = lax.broadcasted_iota(jnp.int32, (LOWF, 256), 0)
                v = lax.broadcasted_iota(jnp.int32, (4 * LOWF, 256), 0)
                at_u.append(jnp.where(u == pos // BLOCK, 1.0, 0.0).astype(BF16))
                at_v.append(jnp.where(v == pos % BLOCK + LOWF * b, 1.0, 0.0).astype(BF16))
            mask[pl.ds(LOWF * i, LOWF), pl.ds(BLOCK * t, BLOCK)] = lax.dot_general(
                jnp.concatenate(at_u, axis=1),
                jnp.concatenate(at_v, axis=1),
                (((1,), (1,)), ((), ())),
                preferred_element_type=F32,
            )

    loads["narrow"].wait()
    low = narrow[1024:1056], narrow[1056:1088]
    turned = narrow[1088:1216, :LOWF], narrow[1216:1344, :LOWF]
    for i in range(3):
        rows = pl.ds(BLOCK * i, BLOCK)
        for name in ("base", "local", "err"):
            loads[name, i].wait()
        for t, (first, width) in enumerate(TILES):
            span = pl.ds(first, width)
            pseudo = base[rows, span] - local[rows, span] + err[rows, span]
            e_ref[rows, span] = pseudo
            diag_t = narrow[0:width], narrow[512 : 512 + width]
            half = three(halves(pseudo), diag_t)
            coef = three(low, halves(half))
            kept[pl.ds(LOWF * i, LOWF), pl.ds(BLOCK * t, BLOCK)] = (
                coef * mask[pl.ds(LOWF * i, LOWF), pl.ds(BLOCK * t, BLOCK)]
            )
    for t in range(4):
        for a in range(2):
            rs_send[4 * a + t] = kept[48 * a : 48 * a + 48, BLOCK * t : BLOCK * t + BLOCK].astype(BF16)

    pl.semaphore_wait(barrier, len(partners))
    scatter = []
    for k in range(7):
        scatter.append(
            pltpu.make_async_remote_copy(
                src_ref=rs_send.at[peers[k]], dst_ref=rs_recv.at[k],
                send_sem=red_send.at[k], recv_sem=red_recv.at[k],
                device_id=peer_device[k], device_id_type=MESH,
            )
        )
        scatter[-1].start()

    loads["wide"].wait()
    diag = wide[0:128], wide[128:256]
    for t, (first, width) in enumerate(TILES):
        spread = three(halves(kept[:, BLOCK * t : BLOCK * t + BLOCK]), (diag[0][:, :width], diag[1][:, :width]))
        for i in range(3):
            back = three(turned, halves(spread[LOWF * i : LOWF * i + LOWF]))
            rows, span = pl.ds(BLOCK * i, BLOCK), pl.ds(first, width)
            e_ref[rows, span] = e_ref[rows, span] - back

    total = rs_send[group].astype(F32)
    for k in range(7):
        scatter[k].wait()
        total = total + rs_recv[k].astype(F32)
    part[0] = total.astype(BF16)
    far = pltpu.make_async_remote_copy(
        src_ref=part.at[0], dst_ref=part.at[1], send_sem=red_send.at[7], recv_sem=red_recv.at[7],
        device_id=device["far"], device_id_type=MESH,
    )
    far.start()
    far.wait()
    mean[group] = ((part[0].astype(F32) + part[1].astype(F32)) * (1.0 / N_REPLICA)).astype(BF16)
    spread_out = []
    for k in range(7):
        spread_out.append(
            pltpu.make_async_remote_copy(
                src_ref=mean.at[group], dst_ref=mean.at[group],
                send_sem=red_send.at[8 + k], recv_sem=red_recv.at[8 + k],
                device_id=peer_device[k], device_id_type=MESH,
            )
        )
        spread_out[-1].start()
    for copy in spread_out:
        copy.wait()

    loads["mom"].wait()
    own = pl.multiple_of(f * cols, BLOCK)
    for t, (first, width) in enumerate(TILES):
        m_t = jnp.concatenate([mean[t], mean[4 + t]], axis=0)
        spread = mm(m_t, diag[0][:, :width]) + mm(m_t, diag[1][:, :width])
        for i in range(3):
            update = three(turned, halves(spread[LOWF * i : LOWF * i + LOWF]))
            rows, span = pl.ds(BLOCK * i, BLOCK), pl.ds(first, width)
            moved = outer_momentum * mom[rows, span] + update
            m_ref[rows, span] = moved
            weights = base[rows, span] - outer_rate * (update + outer_momentum * moved)
            z_ref[rows, pl.ds(pl.multiple_of(own + first, BLOCK), width)] = weights.astype(BF16)

    odd = x % 2

    class Stage:
        def __init__(self, s):
            start, count, outer, middle = STAGES[s]
            first = start + c * count
            self.s, self.count = s, count
            self.size = {"m": middle, "o": outer, "q": outer}
            self.row = {
                "m": first + outer,
                "o": first + odd * (outer + middle),
                "q": first + (1 - odd) * (outer + middle),
            }
            self.names = {}

        def sem(self, key):
            return in_sem.at[self.s, self.names.setdefault(key, len(self.names))]

        def ref(self, p, dy, dz, h):
            column = (((y + dy + 4) % 4) * 4 + (zl + dz + 4) % 4) * cols
            if h is None:
                span = pl.ds(pl.multiple_of(column, BLOCK), cols)
            else:
                span = pl.ds(pl.multiple_of(column + h * (cols // 2), BLOCK), cols // 2)
            return z_ref.at[pl.ds(pl.multiple_of(self.row[p], 16), self.size[p]), span]

        def copy(self, p, a, b, h, way, recv):
            dy, dz = (a, b) if p != "o" else (b, a)
            ref = self.ref(p, dy, dz, h)
            return pltpu.make_async_remote_copy(
                src_ref=ref, dst_ref=ref, send_sem=out_sem.at[self.s, WAYS.index(way)], recv_sem=recv,
                device_id=device[way], device_id_type=MESH,
            )

        def axes(self, p):
            return ("y", "z") if p == "m" else ("z", "y")

        def send(self, p, a, b, h, axis, sign, key):
            way = self.axes(p)[axis] + sign
            self.copy(p, a, b, h, way, self.sem((p,) + key)).start()

        def arrive(self, p, a, b, h, key):
            self.copy(p, a, b, h, "pair", self.sem((p,) + key)).wait_recv()

        def share(self, p, a, b, h):
            self.copy(p, a, b, h, "pair", pair_sem.at[self.s]).start()
            if p == "o":
                for half, way in ((0, "x+"), (1, "x-")):
                    if h is None or h == half:
                        self.copy(p, a, b, half, way, self.sem(("x", a % 4, b % 4, half))).start()

        def begin(self):
            for p in "mo":
                for sign, back in (("+", "-"), ("-", "+")):
                    self.send(p, 0, 0, None, 0, sign, ("A", back, "full"))
            for p in "mo":
                for sign, back in (("+", "-"), ("-", "+")):
                    self.send(p, 0, 0, None, 1, sign, ("B", 0, back, "full"))

        def first_full(self):
            for p in "mo":
                for sign, back, a, h in (("+", "-", -1, 0), ("-", "+", 1, 1)):
                    self.arrive(p, a, 0, None, ("A", back, "full"))
                    self.send(p, a, 0, h, 0, sign, ("A", back, "half"))
                    for sign2, back2 in (("+", "-"), ("-", "+")):
                        self.send(p, a, 0, None, 1, sign2, ("B", a, back2, "full"))
                    self.share(p, a, 0, None)

        def first_half(self):
            for p in "mo":
                for back, h in (("-", 0), ("+", 1)):
                    self.arrive(p, 2, 0, h, ("A", back, "half"))
                    for sign2, back2 in (("+", "-"), ("-", "+")):
                        self.send(p, 2, 0, h, 1, sign2, ("B", 2, back2, h))
                    self.share(p, 2, 0, h)

        def second_full(self, a):
            for p in "mo":
                for sign, back, b, h in (("+", "-", -1, 0), ("-", "+", 1, 1)):
                    self.arrive(p, a, b, None, ("B", a, back, "full"))
                    self.send(p, a, b, h, 1, sign, ("B", a, back, "half"))
                    self.share(p, a, b, None)

        def second_parts(self, h):
            for p in "mo":
                for sign, back, b, forward in (("+", "-", -1, 0), ("-", "+", 1, 1)):
                    self.arrive(p, 2, b, h, ("B", 2, back, h))
                    if h == forward:
                        self.send(p, 2, b, h, 1, sign, ("B", 2, back, "half"))
                    self.share(p, 2, b, h)

        def second_half(self, a):
            for p in "mo":
                for back, h in (("-", 0), ("+", 1)):
                    self.arrive(p, a, 2, h, ("B", a, back, "half"))
                    self.share(p, a, 2, h)

        def across(self, places):
            for a, b in places:
                for h in (0, 1):
                    ref = self.ref("q", b, a, h)
                    copy = functools.partial(
                        pltpu.make_async_remote_copy, src_ref=ref, dst_ref=ref,
                        send_sem=out_sem.at[self.s, WAYS.index("pair")],
                        device_id=device["pair"], device_id_type=MESH,
                    )
                    copy(recv_sem=self.sem(("x", a % 4, b % 4, h))).wait_recv()
                    copy(recv_sem=pair_sem.at[self.s]).start()

        def finish(self):
            outer, middle = self.size["o"], self.size["m"]
            each = 15 * cols // 2

            def drain(way, rows, columns):
                ref = z_ref.at[pl.ds(0, rows), pl.ds(0, columns)]
                pltpu.make_async_remote_copy(
                    src_ref=ref, dst_ref=ref, send_sem=out_sem.at[self.s, WAYS.index(way)],
                    recv_sem=pair_sem.at[self.s], device_id=device["pair"], device_id_type=MESH,
                ).wait_send()

            for way in ("y+", "y-", "z+", "z-"):
                assert outer == middle
                drain(way, outer, each)
            for way in ("x+", "x-"):
                drain(way, outer, each)
            drain("pair", self.count, 15 * cols)
            ref = z_ref.at[pl.ds(0, self.count), pl.ds(0, 15 * cols)]
            pltpu.make_async_remote_copy(
                src_ref=ref, dst_ref=ref, send_sem=out_sem.at[self.s, WAYS.index("pair")],
                recv_sem=pair_sem.at[self.s], device_id=device["pair"], device_id_type=MESH,
            ).wait_recv()

    stages = [Stage(s) for s in range(len(STAGES))]

    def early(g):
        g.first_full()
        g.second_full(0)
        g.first_half()
        g.across([(-1, 0), (1, 0)])
        g.second_full(-1)
        g.second_full(1)
        g.across([(0, -1), (0, 1), (2, 0)])

    def late(g):
        g.second_half(0)
        g.second_parts(0)
        g.second_parts(1)
        g.across([(-1, -1), (-1, 1), (1, -1), (1, 1)])
        g.second_half(-1)
        g.second_half(1)
        g.second_half(2)
        g.across([(0, 2), (2, -1), (2, 1), (-1, 2), (1, 2), (2, 2)])

    stages[0].begin()
    early(stages[0])
    stages[1].begin()
    late(stages[0])
    early(stages[1])
    late(stages[1])
    for g in stages:
        g.finish()


WAYS = ("y+", "y-", "z+", "z-", "x+", "x-", "pair")


def store(z_ref, e_ref, m_ref, w_out, e_out, m_out, sem):
    rows = z_ref.shape[0] // 8
    copies = [
        pltpu.make_async_copy(z_ref.at[pl.ds(rows * k, rows)], w_out.at[pl.ds(rows * k, rows)], sem.at[k])
        for k in range(8)
    ]
    copies.append(pltpu.make_async_copy(e_ref, e_out.at[0], sem.at[8]))
    copies.append(pltpu.make_async_copy(m_ref, m_out, sem.at[9]))
    for copy in copies:
        copy.start()
    for copy in copies:
        copy.wait()


def body(local_weights, base_weights, error_buffer, momentum, keep_index):
    rows, cols = base_weights.shape
    shards = lax.axis_size("fsdp")
    wide, narrow = tables()
    hbm = pl.BlockSpec(memory_space=pltpu.HBM)
    vmem = pl.BlockSpec(memory_space=pltpu.VMEM)
    z, e, m = pl.pallas_call(
        kernel,
        out_shape=(
            pltpu.VMEM((rows, shards * cols), BF16),
            pltpu.VMEM((rows, cols), F32),
            pltpu.VMEM((rows, cols), F32),
        ),
        in_specs=[hbm] * 7,
        out_specs=[vmem] * 3,
        scratch_shapes=[pltpu.VMEM((rows, cols), F32)] * 4
        + [
            pltpu.VMEM((3, 14, 256), jnp.int32),
            pltpu.VMEM((256, 512), BF16),
            pltpu.VMEM((1344, 128), BF16),
            pltpu.VMEM((96, 512), F32),
            pltpu.VMEM((96, 512), F32),
            pltpu.VMEM((8, 48, 128), BF16),
            pltpu.VMEM((7, 48, 128), BF16),
            pltpu.VMEM((2, 48, 128), BF16),
            pltpu.VMEM((8, 48, 128), BF16),
            pltpu.SemaphoreType.DMA((13,)),
            pltpu.SemaphoreType.DMA((15,)),
            pltpu.SemaphoreType.DMA((15,)),
            pltpu.SemaphoreType.DMA((2, 7)),
            pltpu.SemaphoreType.DMA((2, 80)),
            pltpu.SemaphoreType.DMA((2,)),
        ],
        compiler_params=pltpu.CompilerParams(
            collective_id=1, has_side_effects=True, vmem_limit_bytes=30 << 20
        ),
        name="step",
    )(
        local_weights,
        base_weights,
        error_buffer,
        momentum,
        keep_index.transpose(1, 0, 2),
        jnp.asarray(wide),
        jnp.asarray(narrow),
    )
    weights, new_error, new_momentum = pl.pallas_call(
        store,
        out_shape=(
            jax.ShapeDtypeStruct((rows, shards * cols), BF16),
            jax.ShapeDtypeStruct((1, rows, cols), F32),
            jax.ShapeDtypeStruct((rows, cols), F32),
        ),
        in_specs=[vmem] * 3,
        out_specs=[pl.BlockSpec(memory_space=pl.ANY)] * 3,
        scratch_shapes=[pltpu.SemaphoreType.DMA((10,))],
        compiler_params=pltpu.CompilerParams(vmem_limit_bytes=1 << 20),
        name="store",
    )(z, e, m)
    return new_momentum, new_error, weights


def solution(mesh):
    return jax.shard_map(
        body,
        mesh=mesh,
        in_specs=(
            P("replica", None, "fsdp"),
            P(None, "fsdp"),
            P("replica", None, "fsdp"),
            P(None, "fsdp"),
            P("fsdp", None, None),
        ),
        out_specs=(P(None, "fsdp"), P("replica", None, "fsdp"), P()),
        check_vma=False,
    )
```

```python
import functools

import jax
import jax.numpy as jnp
import ml_dtypes
import numpy as np
from jax import lax
from jax.experimental import pallas as pl
from jax.experimental.pallas import tpu as pltpu
from jax.sharding import PartitionSpec as P

MESH = pl.DeviceIdType.MESH
BLOCK = 128
LOWF = 32
N_REPLICA = 16
F32 = jnp.float32
BF16 = jnp.bfloat16
outer_rate = 0.7
outer_momentum = 0.9
OLD = outer_rate * outer_momentum * outer_momentum
NEW = outer_rate * (1.0 + outer_momentum)

TILES = ((0, 512), (512, 512), (1024, 512), (1536, 256))
STAGES = ((0, 128, 48, 32), (256, 64, 16, 32))
EARLY = 2

WAYS = ("y+", "y-", "z+", "z-", "x+", "x-", "pair")
PLACES = [(a, b) for a in (0, 1, 3, 2) for b in (0, 1, 3, 2)][1:]


def lands(part, a, b, way):
    if way in ("x+", "x-"):
        return "q", a, b
    step = -1 if way[1] == "+" else 1
    if way[0] == "A":
        return part, (a + step) % 4, b
    return part, a, (b + step) % 4


def tasks(stages, k_stage=True, pair="split"):
    todo = []

    def add(name, waits, sends, after=()):
        todo.append((name, tuple(waits), tuple(sends), tuple(after)))

    for s, (_, _, outer, middle) in enumerate(stages):
        parts = [p for p, n in (("m", middle), ("o", outer)) if n]

        def u(p, a, b, h=None):
            return s, p, a % 4, b % 4, h

        own = [(u(p, 0, 0), w + sign) for w in "AB" for p in parts for sign in "+-"]
        add(("own", s), [], own, [("ready", s)])
        for p in parts:

            def x(a, b, way, h=None):
                return [(u(p, a, b, h), way)] if p == "o" else []

            for a, sign, h in ((3, "+", 0), (1, "-", 1)):
                sends = [(u(p, a, 0, h), "A" + sign), (u(p, a, 0), "B+"), (u(p, a, 0), "B-")]
                add(("A", s, p, a), [u(p, a, 0)], sends + x(a, 0, "x" + sign))
                add(("H", s, p, h), [u(p, 2, 0, h)], x(2, 0, "x" + sign, h))
            add(("D", s, p), [], [(u(p, 2, 0), "B+"), (u(p, 2, 0), "B-")], [("H", s, p, 0), ("H", s, p, 1)])
            for a in range(4):
                for b, sign in ((3, "+"), (1, "-")):
                    on = [(u(p, a, b), "B" + sign)] if sign == ("+" if a in (0, 1) else "-") else []
                    add(("B", s, p, a, b), [u(p, a, b)], on + x(a, b, "x" + sign))
                add(("B", s, p, a, 2), [u(p, a, 2)], x(a, 2, "x+" if a in (0, 1) else "x-"))
        for dy, dz in PLACES:
            done = []
            for p in parts:
                a, b = (dy, dz) if p == "m" else (dz, dy)
                done.append(("D", s, p) if (a, b) == (2, 0) else ("A", s, p, a) if b == 0 else ("B", s, p, a, b))
            hs = (0, 1) if (dz, dy) == (2, 0) else (None,)
            waits = [u("q", dz, dy, h) for h in hs] if outer else []
            if pair == "all" or not outer:
                add(("P", s, dy, dz), waits, [(u("all", dy, dz), "pair")], done)
            else:
                add(("PM", s, dy, dz), [], [(u("mo", dy, dz), "pair")], done)
                add(("PQ", s, dy, dz), waits, [(u("q", dz, dy), "pair")])
    if k_stage:
        def u(a, b):
            return 0, "k", a % 4, b % 4, None

        add(("own", "k"), [], [(u(0, 0), w + sign) for w in "AB" for sign in "+-"], [("ready", "k")])
        names = []
        for a, sends in ((3, [(u(3, 0), "A+")]), (1, []), (2, [])):
            add(("A", "k", a), [u(a, 0)], sends + [(u(a, 0), "B+"), (u(a, 0), "B-")])
            names.append(("A", "k", a))
        for a in range(4):
            for b, sign in ((3, "+"), (1, "-")):
                on = [(u(a, b), "B" + sign)] if sign == ("+" if a in (0, 1) else "-") else []
                add(("B", "k", a, b), [u(a, b)], on)
            add(("B", "k", a, 2), [u(a, 2)], [])
            names += [("B", "k", a, b) for b in (1, 2, 3)]
        add(("P", "k"), [], [((0, "k", "all", 0, None), "pair")], names)
    return todo


def rows_of(stages, unit):
    s, p, _, _, h = unit
    _, count, outer, middle = stages[s]
    n = {"m": middle, "o": outer, "q": outer, "all": count, "mo": outer + middle, "k": LOWF * 512 / 1792}[p]
    if p == "k" and unit[2] == "all":
        n *= 16
    return n * (1 if h is None else 0.5)


def order(stages, chain, k_stage=True, pair="split", cs=0.09, cw=0.05, lat=1.0, rate=45.5e3, prate=500e3, t0=0.0):
    todo = tasks(stages, k_stage, pair)
    for n, (name, cost, gap) in enumerate(chain):
        todo.append((name, (), (), (chain[n - 1][0],) if n else ()))
    cost = {name: (c, gap) for name, c, gap in chain}
    rank = {"own": 0, "A": 1, "H": 1, "D": 1, "B": 2, "PM": 4, "PQ": 4, "P": 4}
    arrival, free, done, t, out, left = {}, {}, {}, t0, [], list(todo)
    while left:
        best = None
        for n, (name, waits, sends, after) in enumerate(left):
            if any(k not in done for k in after) or any(k not in arrival for k in waits):
                continue
            ready = max([done[k] for k in after] + [arrival[k] for k in waits] + [0])
            r = 3 if name in cost else rank[name[0]]
            if r == 2 and not sends: r = 4
            key = (max(ready, t), r, ready, n)
            if best is None or key < best[0]:
                best = (key, n)
        key, n = best
        name, waits, sends, after = left.pop(n)
        t = max(t, key[0])
        gap = 0
        if name in cost:
            t += cost[name][0]
            gap = cost[name][1]
        t += cw * len(waits)
        for unit, way in sends:
            t += cs
            s, p, a, b, h = unit
            lane = way
            if way[0] in "AB":
                first = p in ("m", "k")
                lane = ("y" if (way[0] == "A") == first else "z") + way[1]
            size = rows_of(stages, unit) * 1792 * 2
            start = max(t, free.get(lane, 0))
            free[lane] = start + size / (prate if way == "pair" else rate)
            if way == "pair":
                arrival["pair", s] = max(arrival.get(("pair", s), 0), free[lane] + lat)
            else:
                q, a2, b2 = lands(p, a, b, way)
                arrival[s, q, a2, b2, h] = free[lane] + lat
        done[name] = t + gap
        out.append((name, waits, sends))
    return out


def split(values):
    high = values.astype(ml_dtypes.bfloat16)
    low = (values - high.astype(np.float64)).astype(ml_dtypes.bfloat16)
    return high, low


def tables():
    u = np.arange(LOWF, dtype=np.float64)[:, None]
    a = np.arange(BLOCK, dtype=np.float64)[None, :]
    norm = np.where(u == 0, np.sqrt(1.0 / BLOCK), np.sqrt(2.0 / BLOCK))
    low = norm * np.cos(np.pi * (2 * a + 1) * u / (2 * BLOCK))
    diag = np.kron(np.eye(4), low)
    wide = np.concatenate(split(diag), axis=0)
    wide = np.concatenate([wide[:, BLOCK * n : BLOCK * n + BLOCK] for n in range(4)], axis=0)
    high, rest = split(low.T)
    turned = np.concatenate([high, rest, high, np.zeros_like(high)], axis=1)
    narrow = np.concatenate(split(diag.T) + split(low) + (turned,), axis=0)
    return wide, narrow


def mm(a, b):
    return jnp.dot(a, b, preferred_element_type=F32)


def halves(v):
    high = v.astype(BF16)
    return high, (v - high.astype(F32)).astype(BF16)


def three(a, b):
    return mm(a[0], b[0]) + (mm(a[1], b[0]) + mm(a[0], b[1]))


def diagonal(wide, width):
    return jnp.concatenate([wide[256 * n : 256 * n + 256] for n in range(width // BLOCK)], axis=1)


def columns_back(coef, diag):
    return mm(jnp.concatenate([coef, coef], axis=1), diag)


def rows_back(turned, spread):
    high, rest = halves(spread)
    return mm(turned, jnp.concatenate([high, high, rest], axis=0))


def kernel(
    local_hbm, base_hbm, err_hbm, mom_hbm, keep_hbm, wide_hbm, narrow_hbm,
    z_ref, e_ref, m_ref, coef_ref,
    local, base, err, mom, keep, wide, narrow,
    mask, kept, rs_send, rs_recv, part, mean,
    load_sem, red_send, red_recv, out_sem, in_sem,
):
    r, f = lax.axis_index("replica"), lax.axis_index("fsdp")
    x, zh, c = r // 4, (r // 2) % 2, r % 2
    y, zl = f // 4, f % 4
    z = zh * 4 + zl
    cols = e_ref.shape[1]
    group = x * 2 + c
    odd = x % 2

    def at(x_, y_, z_, c_):
        return ((x_ * 2 + z_ // 4) * 2 + c_, y_ * 4 + z_ % 4)

    device = {
        "x+": at((x + 1) % 4, y, z, c), "x-": at((x + 3) % 4, y, z, c),
        "y+": at(x, (y + 1) % 4, z, c), "y-": at(x, (y + 3) % 4, z, c),
        "z+": at(x, y, (z + 1) % 8, c), "z-": at(x, y, (z + 7) % 8, c),
        "far": at(x, y, (z + 4) % 8, c), "pair": at(x, y, z, 1 - c),
    }
    for sign in "+-":
        one, two = device["y" + sign], device["z" + sign]
        device["k", "A" + sign] = tuple(p * (1 - c) + q * c for p, q in zip(one, two, strict=True))
        device["k", "B" + sign] = tuple(p * c + q * (1 - c) for p, q in zip(one, two, strict=True))
    peers = [(group + k) % 8 for k in range(1, 8)]
    peer_device = [at(p // 2, y, z, p % 2) for p in peers]

    loads = {}

    def load(name, src, dst):
        loads[name] = pltpu.make_async_copy(src, dst, load_sem.at[len(loads)])
        loads[name].start()

    blocks = [pl.ds(BLOCK * i, BLOCK) for i in range(3)]
    for i in range(EARLY):
        load(("base", i), base_hbm.at[blocks[i]], base.at[blocks[i]])
        load(("mom", i), mom_hbm.at[blocks[i]], mom.at[blocks[i]])
    load("keep", keep_hbm, keep)
    load("narrow", narrow_hbm, narrow)
    for i in range(3):
        load(("local", i), local_hbm.at[0, blocks[i]], local.at[blocks[i]])
        load(("err", i), err_hbm.at[0, blocks[i]], err.at[blocks[i]])
        if i >= EARLY:
            load(("base", i), base_hbm.at[blocks[i]], base.at[blocks[i]])
    load("wide", wide_hbm, wide)
    for i in range(EARLY, 3):
        load(("mom", i), mom_hbm.at[blocks[i]], mom.at[blocks[i]])

    barrier = pltpu.get_barrier_semaphore()
    partners = [device[k] for k in ("y+", "y-", "z+", "z-", "far")] + peer_device
    for d in partners:
        pl.semaphore_signal(barrier, inc=1, device_id=d, device_id_type=MESH)
    own = pl.multiple_of(f * cols, BLOCK)

    def own_columns(t):
        first, width = TILES[t]
        return pl.ds(pl.multiple_of(own + first, BLOCK), width)

    def without_update():
        for i in range(EARLY):
            loads["base", i].wait()
            loads["mom", i].wait()
            for t, (first, width) in enumerate(TILES):
                span = pl.ds(first, width)
                z_ref[blocks[i], own_columns(t)] = (base[blocks[i], span] - OLD * mom[blocks[i], span]).astype(BF16)
        pl.semaphore_wait(barrier, len(partners))

    def positions(i):
        if i == 0:
            loads["keep"].wait()
        for t, (_, width) in enumerate(TILES):
            at_u, at_v = [], []
            for b in range(width // BLOCK):
                pos = keep[i, pl.ds(4 * t + b, 1), :]
                u = lax.broadcasted_iota(jnp.int32, (LOWF, 256), 0)
                v = lax.broadcasted_iota(jnp.int32, (4 * LOWF, 256), 0)
                at_u.append(jnp.where(u == pos // BLOCK, 1.0, 0.0).astype(BF16))
                at_v.append(jnp.where(v == pos % BLOCK + LOWF * b, 1.0, 0.0).astype(BF16))
            mask[pl.ds(LOWF * i, LOWF), pl.ds(BLOCK * t, BLOCK)] = lax.dot_general(
                jnp.concatenate(at_u, axis=1),
                jnp.concatenate(at_v, axis=1),
                (((1,), (1,)), ((), ())),
                preferred_element_type=F32,
            )

    def encode(i):
        if i == 0:
            loads["narrow"].wait()
        for name in ("base", "local", "err") if i >= EARLY else ("local", "err"):
            loads[name, i].wait()
        low = narrow[1024:1056], narrow[1056:1088]
        for t, (first, width) in enumerate(TILES):
            span = pl.ds(first, width)
            pseudo = base[blocks[i], span] - local[blocks[i], span] + err[blocks[i], span]
            e_ref[blocks[i], span] = pseudo
            half = three(halves(pseudo), (narrow[0:width], narrow[512 : 512 + width]))
            coef = three(low, halves(half))
            place = pl.ds(LOWF * i, LOWF), pl.ds(BLOCK * t, BLOCK)
            kept[place] = coef * mask[place]

    def travel(src, dst, n, device_id):
        copy = pltpu.make_async_remote_copy(
            src_ref=src, dst_ref=dst, send_sem=red_send.at[n], recv_sem=red_recv.at[n],
            device_id=device_id, device_id_type=MESH,
        )
        copy.start()
        return copy

    moving = {}

    def scatter():
        for t in range(4):
            for a in range(2):
                rs_send[4 * a + t] = kept[48 * a : 48 * a + 48, BLOCK * t : BLOCK * t + BLOCK].astype(BF16)
        moving["scatter"] = [travel(rs_send.at[peers[k]], rs_recv.at[k], k, peer_device[k]) for k in range(7)]

    def far():
        total = rs_send[group].astype(F32)
        for k in range(7):
            moving["scatter"][k].wait()
            total = total + rs_recv[k].astype(F32)
        part[0] = total.astype(BF16)
        moving["far"] = travel(part.at[0], part.at[1], 7, device["far"])

    def average():
        moving["far"].wait()
        mean[group] = ((part[0].astype(F32) + part[1].astype(F32)) * (1.0 / N_REPLICA)).astype(BF16)
        moving["mean"] = [travel(mean.at[group], mean.at[group], 8 + k, peer_device[k]) for k in range(7)]

    def averaged():
        for copy in moving["mean"]:
            copy.wait()
        for t in range(4):
            place = pl.ds(BLOCK * t, BLOCK)
            coef_ref[c, f, 0:16, place] = mean[t, pl.ds(pl.multiple_of(c * 32, 16), 16), :]
            coef_ref[c, f, 16:32, place] = mean[t + 4 * c, pl.ds(pl.multiple_of((1 - c) * 16, 16), 16), :]

    def residual(t):
        if t == 0:
            loads["wide"].wait()
        first, width = TILES[t]
        diag, span = diagonal(wide, width), pl.ds(first, width)
        high, rest = halves(kept[:, BLOCK * t : BLOCK * t + BLOCK])
        spread = columns_back(high, diag) + mm(rest, diag[:BLOCK])
        for i in range(3):
            back = rows_back(narrow[1088:1216, : 3 * LOWF], spread[LOWF * i : LOWF * i + LOWF])
            e_ref[blocks[i], span] = e_ref[blocks[i], span] - back

    def step(t):
        if t == 0:
            for i in range(EARLY, 3):
                loads["mom", i].wait()
        first, width = TILES[t]
        diag, span = diagonal(wide, width), pl.ds(first, width)
        spread = columns_back(jnp.concatenate([mean[t], mean[4 + t]], axis=0), diag)
        for i in range(3):
            update = rows_back(narrow[1088:1216, : 3 * LOWF], spread[LOWF * i : LOWF * i + LOWF])
            moved = outer_momentum * mom[blocks[i], span] + update
            m_ref[blocks[i], span] = moved
            if i >= EARLY:
                weights = base[blocks[i], span] - outer_rate * (update + outer_momentum * moved)
                z_ref[blocks[i], own_columns(t)] = weights.astype(BF16)

    nothing = lambda: None
    chain = [(("ready", 0), without_update, 2.6, 0)]
    chain += [(("mask", i), functools.partial(positions, i), 0.8, 0) for i in range(3)]
    chain += [(("encode", i), functools.partial(encode, i), 0.8, 0) for i in range(3)]
    chain += [("scatter", scatter, 0.9, 0)]
    chain += [(("residual", t), functools.partial(residual, t), 0.6, 1.5 * t) for t in (0, 1)]
    chain += [("far", far, 0.8, 0)]
    chain += [(("residual", t), functools.partial(residual, t), 0.6, 3.0 * (t - 2)) for t in (2, 3)]
    chain += [("average", average, 0.9, 2.5), (("ready", "k"), averaged, 0.5, 0)]
    chain += [(("update", t), functools.partial(step, t), 0.7, 0) for t in range(4)]
    chain += [(("ready", 1), nothing, 0, 0)]
    compute = {name: run for name, run, _, _ in chain}

    arrivals, departures, sent, received = {}, {}, {}, {}

    def index(table, key):
        return table.setdefault(key, len(table))

    def copy(unit, way, recv_key):
        s, p, a, b, h = unit
        if p == "k":
            if a == "all":
                ref, rows, width = coef_ref.at[c], 16, 16
            else:
                dy, dz = a + c * (b - a), b + c * (a - b)
                shard = ((y + dy) % 4) * 4 + (zl + dz) % 4
                ref, rows, width = coef_ref.at[c, shard], 16, 1
            target = device["pair"] if way == "pair" else device["k", way]
        else:
            start, count, outer, middle = STAGES[s]
            top = start + c * count
            size = {"m": middle, "o": outer, "q": outer, "mo": outer + middle}
            row = {
                "m": top + outer, "o": top + odd * (outer + middle),
                "q": top + (1 - odd) * (outer + middle), "mo": top + odd * outer,
            }
            dy, dz = (a, b) if p in ("m", "mo") else (b, a)
            column = (((y + dy) % 4) * 4 + (zl + dz) % 4) * cols + (h or 0) * (cols // 2)
            rows, width = size[p], cols if h is None else cols // 2
            ref = z_ref.at[pl.ds(pl.multiple_of(row[p], 16), rows), pl.ds(pl.multiple_of(column, BLOCK), width)]
            axes = {"A": "yz"[p == "o"], "B": "zy"[p == "o"]}
            target = device[axes[way[0]] + way[1] if way[0] in "AB" else way]
        out = s, p, way
        made = pltpu.make_async_remote_copy(
            src_ref=ref, dst_ref=ref, send_sem=out_sem.at[index(departures, out)],
            recv_sem=in_sem.at[index(arrivals, recv_key)], device_id=target, device_id_type=MESH,
        )
        return made, out, rows, width

    def send(unit, way):
        s, p, a, b, h = unit
        key = (s, p, "pair") if way == "pair" else (s,) + lands(p, a, b, way) + (h,)
        made, out, rows, width = copy(unit, way, key)
        sent[out] = (rows, sent.get(out, (rows, 0))[1] + width)
        if way == "pair":
            received[key] = sent[out]
        made.start()

    def arrive(unit):
        copy(unit, "pair", unit)[0].wait_recv()

    for name, waits, sends in order(STAGES, [(n, cost, gap) for n, _, cost, gap in chain]):
        for unit in waits:
            arrive(unit)
        if name in compute:
            compute[name]()
        for unit, way in sends:
            send(unit, way)

    def drain(p, rows, width, out_key, in_key):
        if p == "k":
            ref = coef_ref.at[0, pl.ds(0, width)]
        else:
            ref = z_ref.at[pl.ds(0, rows), pl.ds(0, width)]
        return pltpu.make_async_remote_copy(
            src_ref=ref, dst_ref=ref, send_sem=out_sem.at[departures[out_key]],
            recv_sem=in_sem.at[arrivals[in_key]], device_id=device["pair"], device_id_type=MESH,
        )

    some = next(iter(received))
    for out, (rows, width) in sent.items():
        drain(out[1], rows, width, out, some).wait_send()
    for key, (rows, width) in received.items():
        drain(key[1], rows, width, key, key).wait_recv()


def store(
    z_ref, e_ref, m_ref, coef_ref, wide_hbm, narrow_hbm, w_out, e_out, m_out,
    wide, turned, spread, slots, sem, slot_sem,
):
    cols = e_ref.shape[1]
    tables = [
        pltpu.make_async_copy(wide_hbm, wide, sem.at[10]),
        pltpu.make_async_copy(narrow_hbm.at[pl.ds(1088, BLOCK)], turned, sem.at[11]),
    ]
    copies = [
        pltpu.make_async_copy(
            z_ref.at[pl.ds(EARLY * BLOCK + 16 * k, 16)], w_out.at[pl.ds(EARLY * BLOCK + 16 * k, 16)], sem.at[k]
        )
        for k in range(8)
    ]
    copies.append(pltpu.make_async_copy(e_ref, e_out.at[0], sem.at[8]))
    copies.append(pltpu.make_async_copy(m_ref, m_out, sem.at[9]))
    for copy in tables + copies:
        copy.start()
    for copy in tables:
        copy.wait()
    rows = pl.ds(0, EARLY * BLOCK)
    shards = coef_ref.shape[1]

    def out(slot, shard):
        span = pl.ds(pl.multiple_of(shard * cols, BLOCK), cols)
        return pltpu.make_async_copy(slots.at[slot], w_out.at[rows, span], slot_sem.at[slot])

    for i in range(EARLY):
        for t, (first, width) in enumerate(TILES):
            coef = coef_ref[i, :, :, pl.ds(BLOCK * t, BLOCK)].reshape(shards * LOWF, BLOCK)
            spread[i, :, pl.ds(first, width)] = columns_back(coef, diagonal(wide, width)).astype(BF16)

    table = turned[:, : 2 * LOWF]
    none = jnp.zeros_like(table)
    both = jnp.concatenate(
        [jnp.concatenate([table, none], axis=1), jnp.concatenate([none, table], axis=1)], axis=0
    )

    def place(slot, shard, again):
        if again is not None:
            pl.when(again)(lambda: out(slot, shard).wait())
        lines = pl.ds(pl.multiple_of(shard * LOWF, LOWF), LOWF)
        for first, width in TILES:
            span = pl.ds(first, width)
            one, two = spread[0, lines, span], spread[1, lines, span]
            update = mm(both, jnp.concatenate([one, one, two, two], axis=0))
            before = z_ref[rows, pl.ds(pl.multiple_of(shard * cols + first, BLOCK), width)].astype(F32)
            slots[slot, :, span] = (before - NEW * update).astype(BF16)
        out(slot, shard).start()

    n = slots.shape[0]

    def turn(k, carry):
        for slot in range(n):
            place(slot, k * n + slot, k > 0)
        return carry

    lax.fori_loop(0, shards // n, turn, 0)
    for slot in range(n):
        out(slot, shards - n + slot).wait()
    for copy in copies:
        copy.wait()


def body(local_weights, base_weights, error_buffer, momentum, keep_index):
    rows, cols = base_weights.shape
    shards = lax.axis_size("fsdp")
    wide, narrow = (jnp.asarray(table) for table in tables())
    hbm = pl.BlockSpec(memory_space=pltpu.HBM)
    vmem = pl.BlockSpec(memory_space=pltpu.VMEM)
    z, e, m, coef = pl.pallas_call(
        kernel,
        out_shape=(
            pltpu.VMEM((rows, shards * cols), BF16),
            pltpu.VMEM((rows, cols), F32),
            pltpu.VMEM((rows, cols), F32),
            pltpu.VMEM((EARLY, shards, LOWF, 512), BF16),
        ),
        in_specs=[hbm] * 7,
        out_specs=[vmem] * 4,
        scratch_shapes=[pltpu.VMEM((rows, cols), F32)] * 4
        + [
            pltpu.VMEM((3, 14, 256), jnp.int32),
            pltpu.VMEM((1024, 128), BF16),
            pltpu.VMEM((1216, 128), BF16),
            pltpu.VMEM((96, 512), F32),
            pltpu.VMEM((96, 512), F32),
            pltpu.VMEM((8, 48, 128), BF16),
            pltpu.VMEM((7, 48, 128), BF16),
            pltpu.VMEM((2, 48, 128), BF16),
            pltpu.VMEM((8, 48, 128), BF16),
            pltpu.SemaphoreType.DMA((15,)),
            pltpu.SemaphoreType.DMA((15,)),
            pltpu.SemaphoreType.DMA((15,)),
            pltpu.SemaphoreType.DMA((48,)),
            pltpu.SemaphoreType.DMA((192,)),
        ],
        compiler_params=pltpu.CompilerParams(
            collective_id=1, has_side_effects=True, vmem_limit_bytes=35 << 20
        ),
        name="step",
    )(
        local_weights,
        base_weights,
        error_buffer,
        momentum,
        keep_index.transpose(1, 0, 2),
        wide,
        narrow,
    )
    weights, new_error, new_momentum = pl.pallas_call(
        store,
        out_shape=(
            jax.ShapeDtypeStruct((rows, shards * cols), BF16),
            jax.ShapeDtypeStruct((1, rows, cols), F32),
            jax.ShapeDtypeStruct((rows, cols), F32),
        ),
        in_specs=[vmem] * 4 + [hbm] * 2,
        out_specs=[pl.BlockSpec(memory_space=pl.ANY)] * 3,
        scratch_shapes=[
            pltpu.VMEM((1024, 128), BF16),
            pltpu.VMEM((128, 128), BF16),
            pltpu.VMEM((EARLY, shards * LOWF, cols), BF16),
            pltpu.VMEM((2, EARLY * BLOCK, cols), BF16),
            pltpu.SemaphoreType.DMA((12,)),
            pltpu.SemaphoreType.DMA((2,)),
        ],
        compiler_params=pltpu.CompilerParams(vmem_limit_bytes=6 << 20),
        name="store",
    )(z, e, m, coef, wide, narrow)
    return new_momentum, new_error, weights


def solution(mesh):
    return jax.shard_map(
        body,
        mesh=mesh,
        in_specs=(
            P("replica", None, "fsdp"),
            P(None, "fsdp"),
            P("replica", None, "fsdp"),
            P(None, "fsdp"),
            P("fsdp", None, None),
        ),
        out_specs=(P(None, "fsdp"), P("replica", None, "fsdp"), P()),
        check_vma=False,
    )
```

```python
import functools

import jax
import jax.numpy as jnp
import ml_dtypes
import numpy as np
from jax import lax
from jax.experimental import pallas as pl
from jax.experimental.pallas import tpu as pltpu
from jax.sharding import PartitionSpec as P

MESH = pl.DeviceIdType.MESH
BLOCK = 128
LOWF = 32
N_REPLICA = 16
F32 = jnp.float32
BF16 = jnp.bfloat16
outer_rate = 0.7
outer_momentum = 0.9
OLD = outer_rate * outer_momentum * outer_momentum
NEW = outer_rate * (1.0 + outer_momentum)

TILES = ((0, 512), (512, 512), (1024, 512), (1536, 256))
STAGES = ((0, 128, 48, 32), (256, 48, 16, 16), (352, 16, 0, 16))
EARLY = 2

WAYS = ("y+", "y-", "z+", "z-", "x+", "x-", "pair")
PLACES = [(a, b) for a in (0, 1, 3, 2) for b in (0, 1, 3, 2)][1:]


def lands(part, a, b, way):
    if way in ("x+", "x-"):
        return "q", a, b
    step = -1 if way[1] == "+" else 1
    if way[0] == "A":
        return part, (a + step) % 4, b
    return part, a, (b + step) % 4


def tasks(stages, k_stage=True, pair="split"):
    todo = []

    def add(name, waits, sends, after=()):
        todo.append((name, tuple(waits), tuple(sends), tuple(after)))

    for s, (_, _, outer, middle) in enumerate(stages):
        parts = [p for p, n in (("m", middle), ("o", outer)) if n]

        def u(p, a, b, h=None):
            return s, p, a % 4, b % 4, h

        own = [(u(p, 0, 0), w + sign) for w in "AB" for p in parts for sign in "+-"]
        add(("own", s), [], own, [("ready", s)])
        for p in parts:

            def x(a, b, way, h=None):
                return [(u(p, a, b, h), way)] if p == "o" else []

            for a, sign, h in ((3, "+", 0), (1, "-", 1)):
                sends = [(u(p, a, 0, h), "A" + sign), (u(p, a, 0), "B+"), (u(p, a, 0), "B-")]
                add(("A", s, p, a), [u(p, a, 0)], sends + x(a, 0, "x" + sign))
                add(("H", s, p, h), [u(p, 2, 0, h)], x(2, 0, "x" + sign, h))
            add(("D", s, p), [], [(u(p, 2, 0), "B+"), (u(p, 2, 0), "B-")], [("H", s, p, 0), ("H", s, p, 1)])
            for a in range(4):
                for b, sign in ((3, "+"), (1, "-")):
                    on = [(u(p, a, b), "B" + sign)] if sign == ("+" if a in (0, 1) else "-") else []
                    add(("B", s, p, a, b), [u(p, a, b)], on + x(a, b, "x" + sign))
                add(("B", s, p, a, 2), [u(p, a, 2)], x(a, 2, "x+" if a in (0, 1) else "x-"))
        for dy, dz in PLACES:
            done = []
            for p in parts:
                a, b = (dy, dz) if p == "m" else (dz, dy)
                done.append(("D", s, p) if (a, b) == (2, 0) else ("A", s, p, a) if b == 0 else ("B", s, p, a, b))
            hs = (0, 1) if (dz, dy) == (2, 0) else (None,)
            waits = [u("q", dz, dy, h) for h in hs] if outer else []
            if pair == "all" or not outer:
                add(("P", s, dy, dz), waits, [(u("all", dy, dz), "pair")], done)
            else:
                add(("PM", s, dy, dz), [], [(u("mo", dy, dz), "pair")], done)
                add(("PQ", s, dy, dz), waits, [(u("q", dz, dy), "pair")])
    if k_stage:
        def u(a, b):
            return 0, "k", a % 4, b % 4, None

        add(("own", "k"), [], [(u(0, 0), w + sign) for w in "AB" for sign in "+-"], [("ready", "k")])
        names = []
        for a, sends in ((3, [(u(3, 0), "A+")]), (1, []), (2, [])):
            add(("A", "k", a), [u(a, 0)], sends + [(u(a, 0), "B+"), (u(a, 0), "B-")])
            names.append(("A", "k", a))
        for a in range(4):
            for b, sign in ((3, "+"), (1, "-")):
                on = [(u(a, b), "B" + sign)] if sign == ("+" if a in (0, 1) else "-") else []
                add(("B", "k", a, b), [u(a, b)], on)
            add(("B", "k", a, 2), [u(a, 2)], [])
            names += [("B", "k", a, b) for b in (1, 2, 3)]
        add(("P", "k"), [], [((0, "k", "all", 0, None), "pair")], names)
    return todo


def rows_of(stages, unit):
    s, p, _, _, h = unit
    _, count, outer, middle = stages[s]
    n = {"m": middle, "o": outer, "q": outer, "all": count, "mo": outer + middle, "k": LOWF * 512 / 1792}[p]
    if p == "k" and unit[2] == "all":
        n *= 16
    return n * (1 if h is None else 0.5)


def order(stages, chain, k_stage=True, pair="split", cs=0.09, cw=0.05, lat=3.0, rate=45.5e3, prate=500e3, t0=0.0):
    todo = tasks(stages, k_stage, pair)
    for n, (name, cost, gap) in enumerate(chain):
        todo.append((name, (), (), (chain[n - 1][0],) if n else ()))
    cost = {name: (c, gap) for name, c, gap in chain}
    rank = {"own": 0, "A": 1, "H": 1, "D": 1, "B": 2, "PM": 4, "PQ": 4, "P": 4}
    arrival, free, done, t, out, left = {}, {}, {}, t0, [], list(todo)
    while left:
        best = None
        for n, (name, waits, sends, after) in enumerate(left):
            if any(k not in done for k in after) or any(k not in arrival for k in waits):
                continue
            ready = max([done[k] for k in after] + [arrival[k] for k in waits] + [0])
            r = 3 if name in cost else rank[name[0]]
            if r == 2 and not sends: r = 4
            key = (max(ready, t), r, ready, n)
            if best is None or key < best[0]:
                best = (key, n)
        key, n = best
        name, waits, sends, after = left.pop(n)
        t = max(t, key[0])
        gap = 0
        if name in cost:
            t += cost[name][0]
            gap = cost[name][1]
        t += cw * len(waits)
        for unit, way in sends:
            t += cs
            s, p, a, b, h = unit
            lane = way
            if way[0] in "AB":
                first = p in ("m", "k")
                lane = ("y" if (way[0] == "A") == first else "z") + way[1]
            size = rows_of(stages, unit) * 1792 * 2
            start = max(t, free.get(lane, 0))
            free[lane] = start + size / (prate if way == "pair" else rate)
            if way == "pair":
                arrival["pair", s] = max(arrival.get(("pair", s), 0), free[lane] + lat)
            else:
                q, a2, b2 = lands(p, a, b, way)
                arrival[s, q, a2, b2, h] = free[lane] + lat
        done[name] = t + gap
        out.append((name, waits, sends))
    return out


def split(values):
    high = values.astype(ml_dtypes.bfloat16)
    low = (values - high.astype(np.float64)).astype(ml_dtypes.bfloat16)
    return high, low


def tables():
    u = np.arange(LOWF, dtype=np.float64)[:, None]
    a = np.arange(BLOCK, dtype=np.float64)[None, :]
    norm = np.where(u == 0, np.sqrt(1.0 / BLOCK), np.sqrt(2.0 / BLOCK))
    low = norm * np.cos(np.pi * (2 * a + 1) * u / (2 * BLOCK))
    step = split(-NEW * low.T)
    diag = np.kron(np.eye(4), low)
    wide = np.concatenate(split(diag), axis=0)
    wide = np.concatenate([wide[:, BLOCK * n : BLOCK * n + BLOCK] for n in range(4)], axis=0)
    high, rest = split(low.T)
    turned = np.concatenate([high, rest, high, np.zeros_like(high)], axis=1)
    step = np.concatenate(step + (np.zeros((BLOCK, 2 * LOWF), ml_dtypes.bfloat16),), axis=1)
    narrow = np.concatenate(split(diag.T) + split(low) + (turned, step), axis=0)
    return wide, narrow


def mm(a, b):
    return jnp.dot(a, b, preferred_element_type=F32)


def halves(v):
    high = v.astype(BF16)
    return high, (v - high.astype(F32)).astype(BF16)


def three(a, b):
    return mm(a[0], b[0]) + (mm(a[1], b[0]) + mm(a[0], b[1]))


def diagonal(wide, width):
    return jnp.concatenate([wide[256 * n : 256 * n + 256] for n in range(width // BLOCK)], axis=1)


def columns_back(coef, diag):
    return mm(jnp.concatenate([coef, coef], axis=1), diag)


def rows_back(turned, spread):
    high, rest = halves(spread)
    return mm(turned, jnp.concatenate([high, high, rest], axis=0))


def kernel(
    local_hbm, base_hbm, err_hbm, mom_hbm, keep_hbm, wide_hbm, narrow_hbm,
    z_ref, e_ref, m_ref, coef_ref,
    local, base, err, mom, keep, wide, narrow,
    mask, kept, rs_send, rs_recv, part, mean,
    load_sem, red_send, red_recv, out_sem, in_sem,
):
    r, f = lax.axis_index("replica"), lax.axis_index("fsdp")
    x, zh, c = r // 4, (r // 2) % 2, r % 2
    y, zl = f // 4, f % 4
    z = zh * 4 + zl
    cols = e_ref.shape[1]
    group = x * 2 + c
    odd = x % 2

    def at(x_, y_, z_, c_):
        return ((x_ * 2 + z_ // 4) * 2 + c_, y_ * 4 + z_ % 4)

    device = {
        "x+": at((x + 1) % 4, y, z, c), "x-": at((x + 3) % 4, y, z, c),
        "y+": at(x, (y + 1) % 4, z, c), "y-": at(x, (y + 3) % 4, z, c),
        "z+": at(x, y, (z + 1) % 8, c), "z-": at(x, y, (z + 7) % 8, c),
        "far": at(x, y, (z + 4) % 8, c), "pair": at(x, y, z, 1 - c),
    }
    for sign in "+-":
        one, two = device["y" + sign], device["z" + sign]
        device["k", "A" + sign] = tuple(p * (1 - c) + q * c for p, q in zip(one, two, strict=True))
        device["k", "B" + sign] = tuple(p * c + q * (1 - c) for p, q in zip(one, two, strict=True))
    peers = [(group + k) % 8 for k in range(1, 8)]
    peer_device = [at(p // 2, y, z, p % 2) for p in peers]

    loads = {}

    def load(name, src, dst):
        loads[name] = pltpu.make_async_copy(src, dst, load_sem.at[len(loads)])
        loads[name].start()

    blocks = [pl.ds(BLOCK * i, BLOCK) for i in range(3)]
    for i in range(EARLY):
        load(("base", i), base_hbm.at[blocks[i]], base.at[blocks[i]])
        load(("mom", i), mom_hbm.at[blocks[i]], mom.at[blocks[i]])
    load("keep", keep_hbm, keep)
    load("narrow", narrow_hbm, narrow)
    for i in range(3):
        load(("local", i), local_hbm.at[0, blocks[i]], local.at[blocks[i]])
        load(("err", i), err_hbm.at[0, blocks[i]], err.at[blocks[i]])
        if i >= EARLY:
            load(("base", i), base_hbm.at[blocks[i]], base.at[blocks[i]])
    load("wide", wide_hbm, wide)
    for i in range(EARLY, 3):
        load(("mom", i), mom_hbm.at[blocks[i]], mom.at[blocks[i]])

    barrier = pltpu.get_barrier_semaphore()
    partners = [device[k] for k in ("y+", "y-", "z+", "z-", "far")] + peer_device
    for d in partners:
        pl.semaphore_signal(barrier, inc=1, device_id=d, device_id_type=MESH)
    own = pl.multiple_of(f * cols, BLOCK)

    def own_columns(t):
        first, width = TILES[t]
        return pl.ds(pl.multiple_of(own + first, BLOCK), width)

    def without_update():
        for i in range(EARLY):
            loads["base", i].wait()
            loads["mom", i].wait()
            for t, (first, width) in enumerate(TILES):
                span = pl.ds(first, width)
                z_ref[blocks[i], own_columns(t)] = (base[blocks[i], span] - OLD * mom[blocks[i], span]).astype(BF16)
        pl.semaphore_wait(barrier, len(partners))

    def positions(i):
        if i == 0:
            loads["keep"].wait()
        for t, (_, width) in enumerate(TILES):
            at_u, at_v = [], []
            for b in range(width // BLOCK):
                pos = keep[i, pl.ds(4 * t + b, 1), :]
                u = lax.broadcasted_iota(jnp.int32, (LOWF, 256), 0)
                v = lax.broadcasted_iota(jnp.int32, (4 * LOWF, 256), 0)
                at_u.append(jnp.where(u == pos // BLOCK, 1.0, 0.0).astype(BF16))
                at_v.append(jnp.where(v == pos % BLOCK + LOWF * b, 1.0, 0.0).astype(BF16))
            mask[pl.ds(LOWF * i, LOWF), pl.ds(BLOCK * t, BLOCK)] = lax.dot_general(
                jnp.concatenate(at_u, axis=1),
                jnp.concatenate(at_v, axis=1),
                (((1,), (1,)), ((), ())),
                preferred_element_type=F32,
            )

    def encode(i):
        if i == 0:
            loads["narrow"].wait()
        for name in ("base", "local", "err") if i >= EARLY else ("local", "err"):
            loads[name, i].wait()
        low = narrow[1024:1056], narrow[1056:1088]
        for t, (first, width) in enumerate(TILES):
            span = pl.ds(first, width)
            pseudo = base[blocks[i], span] - local[blocks[i], span] + err[blocks[i], span]
            e_ref[blocks[i], span] = pseudo
            half = three(halves(pseudo), (narrow[0:width], narrow[512 : 512 + width]))
            coef = three(low, halves(half))
            place = pl.ds(LOWF * i, LOWF), pl.ds(BLOCK * t, BLOCK)
            kept[place] = coef * mask[place]

    def travel(src, dst, n, device_id):
        copy = pltpu.make_async_remote_copy(
            src_ref=src, dst_ref=dst, send_sem=red_send.at[n], recv_sem=red_recv.at[n],
            device_id=device_id, device_id_type=MESH,
        )
        copy.start()
        return copy

    moving = {}

    def scatter():
        for t in range(4):
            for a in range(2):
                rs_send[4 * a + t] = kept[48 * a : 48 * a + 48, BLOCK * t : BLOCK * t + BLOCK].astype(BF16)
        moving["scatter"] = [travel(rs_send.at[peers[k]], rs_recv.at[k], k, peer_device[k]) for k in range(7)]

    def far():
        total = rs_send[group].astype(F32)
        for k in range(7):
            moving["scatter"][k].wait()
            total = total + rs_recv[k].astype(F32)
        part[0] = total.astype(BF16)
        moving["far"] = travel(part.at[0], part.at[1], 7, device["far"])

    def average():
        moving["far"].wait()
        mean[group] = ((part[0].astype(F32) + part[1].astype(F32)) * (1.0 / N_REPLICA)).astype(BF16)
        moving["mean"] = [travel(mean.at[group], mean.at[group], 8 + k, peer_device[k]) for k in range(7)]

    def averaged():
        for copy in moving["mean"]:
            copy.wait()
        for t in range(4):
            place = pl.ds(BLOCK * t, BLOCK)
            coef_ref[c, f, 0:16, place] = mean[t, pl.ds(pl.multiple_of(c * 32, 16), 16), :]
            coef_ref[c, f, 16:32, place] = mean[t + 4 * c, pl.ds(pl.multiple_of((1 - c) * 16, 16), 16), :]

    def residual(t):
        if t == 0:
            loads["wide"].wait()
        first, width = TILES[t]
        diag, span = diagonal(wide, width), pl.ds(first, width)
        high, rest = halves(kept[:, BLOCK * t : BLOCK * t + BLOCK])
        spread = columns_back(high, diag) + mm(rest, diag[:BLOCK])
        for i in range(3):
            back = rows_back(narrow[1088:1216, : 3 * LOWF], spread[LOWF * i : LOWF * i + LOWF])
            e_ref[blocks[i], span] = e_ref[blocks[i], span] - back

    def step(t):
        if t == 0:
            for i in range(EARLY, 3):
                loads["mom", i].wait()
        first, width = TILES[t]
        diag, span = diagonal(wide, width), pl.ds(first, width)
        spread = columns_back(jnp.concatenate([mean[t], mean[4 + t]], axis=0), diag)
        for i in range(3):
            update = rows_back(narrow[1088:1216, : 3 * LOWF], spread[LOWF * i : LOWF * i + LOWF])
            moved = outer_momentum * mom[blocks[i], span] + update
            m_ref[blocks[i], span] = moved
            if i >= EARLY:
                weights = base[blocks[i], span] - outer_rate * (update + outer_momentum * moved)
                z_ref[blocks[i], own_columns(t)] = weights.astype(BF16)

    nothing = lambda: None
    chain = [(("ready", 0), without_update, 2.6, 0)]
    chain += [(("mask", i), functools.partial(positions, i), 0.8, 0) for i in range(3)]
    chain += [(("encode", i), functools.partial(encode, i), 0.8, 0) for i in range(3)]
    chain += [("scatter", scatter, 0.9, 0)]
    chain += [(("residual", t), functools.partial(residual, t), 0.6, 1.5 * t) for t in (0, 1)]
    chain += [("far", far, 0.8, 0)]
    chain += [(("residual", t), functools.partial(residual, t), 0.6, 3.0 * (t - 2)) for t in (2, 3)]
    chain += [("average", average, 0.9, 2.5), (("ready", "k"), averaged, 0.5, 0)]
    chain += [(("update", t), functools.partial(step, t), 0.7, 0) for t in range(4)]
    chain += [(("ready", 1), nothing, 0, 0), (("ready", 2), nothing, 0, 0)]
    compute = {name: run for name, run, _, _ in chain}

    arrivals, departures, sent, received = {}, {}, {}, {}

    def index(table, key):
        return table.setdefault(key, len(table))

    def copy(unit, way, recv_key):
        s, p, a, b, h = unit
        if p == "k":
            if a == "all":
                ref, rows, width = coef_ref.at[c], 16, 16
            else:
                dy, dz = a + c * (b - a), b + c * (a - b)
                shard = ((y + dy) % 4) * 4 + (zl + dz) % 4
                ref, rows, width = coef_ref.at[c, shard], 16, 1
            target = device["pair"] if way == "pair" else device["k", way]
        else:
            start, count, outer, middle = STAGES[s]
            top = start + c * count
            size = {"m": middle, "o": outer, "q": outer, "mo": outer + middle, "all": count}
            row = {
                "m": top + outer, "o": top + odd * (outer + middle),
                "q": top + (1 - odd) * (outer + middle), "mo": top + odd * outer, "all": top,
            }
            dy, dz = (a, b) if p in ("m", "mo", "all") else (b, a)
            column = (((y + dy) % 4) * 4 + (zl + dz) % 4) * cols + (h or 0) * (cols // 2)
            rows, width = size[p], cols if h is None else cols // 2
            ref = z_ref.at[pl.ds(pl.multiple_of(row[p], 16), rows), pl.ds(pl.multiple_of(column, BLOCK), width)]
            axes = {"A": "yz"[p == "o"], "B": "zy"[p == "o"]}
            target = device[axes[way[0]] + way[1] if way[0] in "AB" else way]
        out = s, p, way
        made = pltpu.make_async_remote_copy(
            src_ref=ref, dst_ref=ref, send_sem=out_sem.at[index(departures, out)],
            recv_sem=in_sem.at[index(arrivals, recv_key)], device_id=target, device_id_type=MESH,
        )
        return made, out, rows, width

    def send(unit, way):
        s, p, a, b, h = unit
        key = (s, p, "pair") if way == "pair" else (s,) + lands(p, a, b, way) + (h,)
        made, out, rows, width = copy(unit, way, key)
        sent[out] = (rows, sent.get(out, (rows, 0))[1] + width)
        if way == "pair":
            received[key] = sent[out]
        made.start()

    def arrive(unit):
        copy(unit, "pair", unit)[0].wait_recv()

    for name, waits, sends in order(STAGES, [(n, cost, gap) for n, _, cost, gap in chain]):
        for unit in waits:
            arrive(unit)
        if name in compute:
            compute[name]()
        for unit, way in sends:
            send(unit, way)

    def drain(p, rows, width, out_key, in_key):
        if p == "k":
            ref = coef_ref.at[0, pl.ds(0, width)]
        else:
            ref = z_ref.at[pl.ds(0, rows), pl.ds(0, width)]
        return pltpu.make_async_remote_copy(
            src_ref=ref, dst_ref=ref, send_sem=out_sem.at[departures[out_key]],
            recv_sem=in_sem.at[arrivals[in_key]], device_id=device["pair"], device_id_type=MESH,
        )

    some = next(iter(received))
    for out, (rows, width) in sent.items():
        drain(out[1], rows, width, out, some).wait_send()
    for key, (rows, width) in received.items():
        drain(key[1], rows, width, key, key).wait_recv()


def store(
    z_ref, e_ref, m_ref, coef_ref, wide_hbm, narrow_hbm, w_out, e_out, m_out,
    wide, turned, spread, slots, sem, slot_sem,
):
    cols = e_ref.shape[1]
    tables = [
        pltpu.make_async_copy(wide_hbm, wide, sem.at[3, 0]),
        pltpu.make_async_copy(narrow_hbm.at[pl.ds(1216, BLOCK)], turned, sem.at[3, 1]),
    ]
    shards = coef_ref.shape[1]
    n = slots.shape[0]
    turns = shards // n

    def rest(k):
        pieces = []
        for m, (src, dst, first) in enumerate(((z_ref, w_out, EARLY * BLOCK), (e_ref, e_out.at[0], 0), (m_ref, m_out, 0))):
            height = (src.shape[0] - first) // turns
            lines = pl.ds(pl.multiple_of(first + height * k, 16), height)
            pieces.append(pltpu.make_async_copy(src.at[lines], dst.at[lines], sem.at[m, k]))
        return pieces

    for copy in tables:
        copy.start()
    for copy in tables:
        copy.wait()
    rows = pl.ds(0, EARLY * BLOCK)

    def out(slot, shard):
        span = pl.ds(pl.multiple_of(shard * cols, BLOCK), cols)
        return pltpu.make_async_copy(slots.at[slot], w_out.at[rows, span], slot_sem.at[slot])

    for i in range(EARLY):
        for t, (first, width) in enumerate(TILES):
            coef = coef_ref[i, :, :, pl.ds(BLOCK * t, BLOCK)].reshape(shards * LOWF, BLOCK)
            spread[i, :, pl.ds(first, width)] = columns_back(coef, diagonal(wide, width)).astype(BF16)

    table = turned[:, : 2 * LOWF]
    none = jnp.zeros_like(table)
    both = jnp.concatenate(
        [jnp.concatenate([table, none], axis=1), jnp.concatenate([none, table], axis=1)], axis=0
    )

    def place(slot, shard, again):
        if again is not None:
            pl.when(again)(lambda: out(slot, shard).wait())
        lines = pl.ds(pl.multiple_of(shard * LOWF, LOWF), LOWF)
        for first in range(0, cols, 256):
            span = pl.ds(first, 256)
            one, two = spread[0, lines, span], spread[1, lines, span]
            update = mm(both, jnp.concatenate([one, one, two, two], axis=0))
            before = z_ref[rows, pl.ds(pl.multiple_of(shard * cols + first, BLOCK), 256)].astype(F32)
            slots[slot, :, span] = (before + update).astype(BF16)
        out(slot, shard).start()

    def turn(k, carry):
        for copy in rest(k):
            copy.start()
        for slot in range(n):
            place(slot, k * n + slot, k > 0)
        return carry

    lax.fori_loop(0, turns, turn, 0)
    for slot in range(n):
        out(slot, shards - n + slot).wait()
    for k in range(turns):
        for copy in rest(k):
            copy.wait()


def body(local_weights, base_weights, error_buffer, momentum, keep_index):
    rows, cols = base_weights.shape
    shards = lax.axis_size("fsdp")
    wide, narrow = (jnp.asarray(table) for table in tables())
    hbm = pl.BlockSpec(memory_space=pltpu.HBM)
    vmem = pl.BlockSpec(memory_space=pltpu.VMEM)
    z, e, m, coef = pl.pallas_call(
        kernel,
        out_shape=(
            pltpu.VMEM((rows, shards * cols), BF16),
            pltpu.VMEM((rows, cols), F32),
            pltpu.VMEM((rows, cols), F32),
            pltpu.VMEM((EARLY, shards, LOWF, 512), BF16),
        ),
        in_specs=[hbm] * 7,
        out_specs=[vmem] * 4,
        scratch_shapes=[pltpu.VMEM((rows, cols), F32)] * 4
        + [
            pltpu.VMEM((3, 14, 256), jnp.int32),
            pltpu.VMEM((1024, 128), BF16),
            pltpu.VMEM((1344, 128), BF16),
            pltpu.VMEM((96, 512), F32),
            pltpu.VMEM((96, 512), F32),
            pltpu.VMEM((8, 48, 128), BF16),
            pltpu.VMEM((7, 48, 128), BF16),
            pltpu.VMEM((2, 48, 128), BF16),
            pltpu.VMEM((8, 48, 128), BF16),
            pltpu.SemaphoreType.DMA((15,)),
            pltpu.SemaphoreType.DMA((15,)),
            pltpu.SemaphoreType.DMA((15,)),
            pltpu.SemaphoreType.DMA((48,)),
            pltpu.SemaphoreType.DMA((192,)),
        ],
        compiler_params=pltpu.CompilerParams(
            collective_id=1, has_side_effects=True, vmem_limit_bytes=35 << 20
        ),
        name="step",
    )(
        local_weights,
        base_weights,
        error_buffer,
        momentum,
        keep_index.transpose(1, 0, 2),
        wide,
        narrow,
    )
    weights, new_error, new_momentum = pl.pallas_call(
        store,
        out_shape=(
            jax.ShapeDtypeStruct((rows, shards * cols), BF16),
            jax.ShapeDtypeStruct((1, rows, cols), F32),
            jax.ShapeDtypeStruct((rows, cols), F32),
        ),
        in_specs=[vmem] * 4 + [hbm] * 2,
        out_specs=[pl.BlockSpec(memory_space=pl.ANY)] * 3,
        scratch_shapes=[
            pltpu.VMEM((1024, 128), BF16),
            pltpu.VMEM((128, 128), BF16),
            pltpu.VMEM((EARLY, shards * LOWF, cols), BF16),
            pltpu.VMEM((2, EARLY * BLOCK, cols), BF16),
            pltpu.SemaphoreType.DMA((4, 8)),
            pltpu.SemaphoreType.DMA((2,)),
        ],
        compiler_params=pltpu.CompilerParams(vmem_limit_bytes=6 << 20),
        name="store",
    )(z, e, m, coef, wide, narrow)
    return new_momentum, new_error, weights


def solution(mesh):
    return jax.shard_map(
        body,
        mesh=mesh,
        in_specs=(
            P("replica", None, "fsdp"),
            P(None, "fsdp"),
            P("replica", None, "fsdp"),
            P(None, "fsdp"),
            P("fsdp", None, None),
        ),
        out_specs=(P(None, "fsdp"), P("replica", None, "fsdp"), P()),
        check_vma=False,
    )
```

```python
import functools

import jax
import jax.numpy as jnp
import ml_dtypes
import numpy as np
from jax import lax
from jax.experimental import pallas as pl
from jax.experimental.pallas import tpu as pltpu
from jax.sharding import PartitionSpec as P

MESH = pl.DeviceIdType.MESH
BLOCK = 128
LOWF = 32
N_REPLICA = 16
F32 = jnp.float32
BF16 = jnp.bfloat16
outer_rate = 0.7
outer_momentum = 0.9
OLD = outer_rate * outer_momentum * outer_momentum
NEW = outer_rate * (1.0 + outer_momentum)

TILES = ((0, 512), (512, 512), (1024, 512), (1536, 256))
STAGES = ((0, 128, 48, 32), (256, 48, 16, 16), (352, 16, 0, 16))
EARLY = 2

WAYS = ("y+", "y-", "z+", "z-", "x+", "x-", "pair")
PLACES = [(a, b) for a in (0, 1, 3, 2) for b in (0, 1, 3, 2)][1:]


def lands(part, a, b, way):
    if way in ("x+", "x-"):
        return "q", a, b
    step = -1 if way[1] == "+" else 1
    if way[0] == "A":
        return part, (a + step) % 4, b
    return part, a, (b + step) % 4


def tasks(stages, k_stage=True, pair="split"):
    todo = []

    def add(name, waits, sends, after=()):
        todo.append((name, tuple(waits), tuple(sends), tuple(after)))

    for s, (_, _, outer, middle) in enumerate(stages):
        parts = [p for p, n in (("m", middle), ("o", outer)) if n]

        def u(p, a, b, h=None):
            return s, p, a % 4, b % 4, h

        own = [(u(p, 0, 0), w + sign) for w in "AB" for p in parts for sign in "+-"]
        add(("own", s), [], own, [("ready", s)])
        for p in parts:

            def x(a, b, way, h=None):
                return [(u(p, a, b, h), way)] if p == "o" else []

            for a, sign, h in ((3, "+", 0), (1, "-", 1)):
                sends = [(u(p, a, 0, h), "A" + sign), (u(p, a, 0), "B+"), (u(p, a, 0), "B-")]
                add(("A", s, p, a), [u(p, a, 0)], sends + x(a, 0, "x" + sign))
                add(("H", s, p, h), [u(p, 2, 0, h)], x(2, 0, "x" + sign, h))
            add(("D", s, p), [], [(u(p, 2, 0), "B+"), (u(p, 2, 0), "B-")], [("H", s, p, 0), ("H", s, p, 1)])
            for a in range(4):
                for b, sign in ((3, "+"), (1, "-")):
                    on = [(u(p, a, b), "B" + sign)] if sign == ("+" if a in (0, 1) else "-") else []
                    add(("B", s, p, a, b), [u(p, a, b)], on + x(a, b, "x" + sign))
                add(("B", s, p, a, 2), [u(p, a, 2)], x(a, 2, "x+" if a in (0, 1) else "x-"))
        for dy, dz in PLACES:
            done = []
            for p in parts:
                a, b = (dy, dz) if p == "m" else (dz, dy)
                done.append(("D", s, p) if (a, b) == (2, 0) else ("A", s, p, a) if b == 0 else ("B", s, p, a, b))
            hs = (0, 1) if (dz, dy) == (2, 0) else (None,)
            waits = [u("q", dz, dy, h) for h in hs] if outer else []
            if pair == "all" or not outer:
                add(("P", s, dy, dz), waits, [(u("all", dy, dz), "pair")], done)
            else:
                add(("PM", s, dy, dz), [], [(u("mo", dy, dz), "pair")], done)
                add(("PQ", s, dy, dz), waits, [(u("q", dz, dy), "pair")])
    if k_stage:
        def u(a, b):
            return 0, "k", a % 4, b % 4, None

        add(("own", "k"), [], [(u(0, 0), w + sign) for w in "AB" for sign in "+-"], [("ready", "k")])
        names = []
        for a, sends in ((3, [(u(3, 0), "A+")]), (1, []), (2, [])):
            add(("A", "k", a), [u(a, 0)], sends + [(u(a, 0), "B+"), (u(a, 0), "B-")])
            names.append(("A", "k", a))
        for a in range(4):
            for b, sign in ((3, "+"), (1, "-")):
                on = [(u(a, b), "B" + sign)] if sign == ("+" if a in (0, 1) else "-") else []
                add(("B", "k", a, b), [u(a, b)], on)
            add(("B", "k", a, 2), [u(a, 2)], [])
            names += [("B", "k", a, b) for b in (1, 2, 3)]
        add(("P", "k"), [], [((0, "k", "all", 0, None), "pair")], names)
    return todo


def rows_of(stages, unit):
    s, p, _, _, h = unit
    _, count, outer, middle = stages[s]
    n = {"m": middle, "o": outer, "q": outer, "all": count, "mo": outer + middle, "k": LOWF * 512 / 1792}[p]
    if p == "k" and unit[2] == "all":
        n *= 16
    return n * (1 if h is None else 0.5)


def order(stages, chain, k_stage=True, pair="split", cs=0.09, cw=0.05, lat=3.0, rate=45.5e3, prate=500e3, t0=0.0):
    todo = tasks(stages, k_stage, pair)
    for n, (name, cost, gap) in enumerate(chain):
        todo.append((name, (), (), (chain[n - 1][0],) if n else ()))
    cost = {name: (c, gap) for name, c, gap in chain}
    rank = {"own": 0, "A": 1, "H": 1, "D": 1, "B": 2, "PM": 4, "PQ": 4, "P": 4}
    arrival, free, done, t, out, left = {}, {}, {}, t0, [], list(todo)
    while left:
        best = None
        for n, (name, waits, sends, after) in enumerate(left):
            if any(k not in done for k in after) or any(k not in arrival for k in waits):
                continue
            ready = max([done[k] for k in after] + [arrival[k] for k in waits] + [0])
            r = 3 if name in cost else rank[name[0]]
            if r == 2 and not sends: r = 4
            key = (max(ready, t), r, ready, n)
            if best is None or key < best[0]:
                best = (key, n)
        key, n = best
        name, waits, sends, after = left.pop(n)
        t = max(t, key[0])
        gap = 0
        if name in cost:
            t += cost[name][0]
            gap = cost[name][1]
        t += cw * len(waits)
        for unit, way in sends:
            t += cs
            s, p, a, b, h = unit
            lane = way
            if way[0] in "AB":
                first = p in ("m", "k")
                lane = ("y" if (way[0] == "A") == first else "z") + way[1]
            size = rows_of(stages, unit) * 1792 * 2
            start = max(t, free.get(lane, 0))
            free[lane] = start + size / (prate if way == "pair" else rate)
            if way == "pair":
                arrival["pair", s] = max(arrival.get(("pair", s), 0), free[lane] + lat)
            else:
                q, a2, b2 = lands(p, a, b, way)
                arrival[s, q, a2, b2, h] = free[lane] + lat
        done[name] = t + gap
        out.append((name, waits, sends))
    return out


def split(values):
    high = values.astype(ml_dtypes.bfloat16)
    low = (values - high.astype(np.float64)).astype(ml_dtypes.bfloat16)
    return high, low


def tables():
    u = np.arange(LOWF, dtype=np.float64)[:, None]
    a = np.arange(BLOCK, dtype=np.float64)[None, :]
    norm = np.where(u == 0, np.sqrt(1.0 / BLOCK), np.sqrt(2.0 / BLOCK))
    low = norm * np.cos(np.pi * (2 * a + 1) * u / (2 * BLOCK))
    step = split(-NEW * low.T)
    diag = np.kron(np.eye(4), low)
    wide = np.concatenate(split(diag), axis=0)
    wide = np.concatenate([wide[:, BLOCK * n : BLOCK * n + BLOCK] for n in range(4)], axis=0)
    high, rest = split(low.T)
    turned = np.concatenate([high, rest, high, np.zeros_like(high)], axis=1)
    step = np.concatenate(step + (np.zeros((BLOCK, 2 * LOWF), ml_dtypes.bfloat16),), axis=1)
    narrow = np.concatenate(split(diag.T) + split(low) + (turned, step), axis=0)
    return wide, narrow


def mm(a, b):
    return jnp.dot(a, b, preferred_element_type=F32)


def halves(v):
    high = v.astype(BF16)
    return high, (v - high.astype(F32)).astype(BF16)


def three(a, b):
    return mm(a[0], b[0]) + (mm(a[1], b[0]) + mm(a[0], b[1]))


def diagonal(wide, width):
    return jnp.concatenate([wide[256 * n : 256 * n + 256] for n in range(width // BLOCK)], axis=1)


def columns_back(coef, diag):
    return mm(jnp.concatenate([coef, coef], axis=1), diag)


def rows_back(turned, spread):
    high, rest = halves(spread)
    return mm(turned, jnp.concatenate([high, high, rest], axis=0))


def kernel(
    local_hbm, base_hbm, err_hbm, mom_hbm, keep_hbm, wide_hbm, narrow_hbm,
    z_ref, e_ref, m_ref, coef_ref,
    local, base, err, mom, keep, wide, narrow,
    mask, kept, rs_send, rs_recv, part, mean,
    load_sem, red_send, red_recv, out_sem, in_sem,
):
    r, f = lax.axis_index("replica"), lax.axis_index("fsdp")
    x, zh, c = r // 4, (r // 2) % 2, r % 2
    y, zl = f // 4, f % 4
    z = zh * 4 + zl
    cols = e_ref.shape[1]
    group = x * 2 + c
    odd = x % 2

    def at(x_, y_, z_, c_):
        return ((x_ * 2 + z_ // 4) * 2 + c_, y_ * 4 + z_ % 4)

    device = {
        "x+": at((x + 1) % 4, y, z, c), "x-": at((x + 3) % 4, y, z, c),
        "y+": at(x, (y + 1) % 4, z, c), "y-": at(x, (y + 3) % 4, z, c),
        "z+": at(x, y, (z + 1) % 8, c), "z-": at(x, y, (z + 7) % 8, c),
        "far": at(x, y, (z + 4) % 8, c), "pair": at(x, y, z, 1 - c),
    }
    for sign in "+-":
        one, two = device["y" + sign], device["z" + sign]
        device["k", "A" + sign] = tuple(p * (1 - c) + q * c for p, q in zip(one, two, strict=True))
        device["k", "B" + sign] = tuple(p * c + q * (1 - c) for p, q in zip(one, two, strict=True))
    peers = [(group + k) % 8 for k in range(1, 8)]
    peer_device = [at(p // 2, y, z, p % 2) for p in peers]

    loads = {}

    def load(name, src, dst):
        loads[name] = pltpu.make_async_copy(src, dst, load_sem.at[len(loads)])
        loads[name].start()

    blocks = [pl.ds(BLOCK * i, BLOCK) for i in range(3)]
    for i in range(EARLY):
        load(("base", i), base_hbm.at[blocks[i]], base.at[blocks[i]])
        load(("mom", i), mom_hbm.at[blocks[i]], mom.at[blocks[i]])
    load("keep", keep_hbm, keep)
    load("narrow", narrow_hbm, narrow)
    for i in range(3):
        load(("local", i), local_hbm.at[0, blocks[i]], local.at[blocks[i]])
        load(("err", i), err_hbm.at[0, blocks[i]], err.at[blocks[i]])
        if i >= EARLY:
            load(("base", i), base_hbm.at[blocks[i]], base.at[blocks[i]])
    load("wide", wide_hbm, wide)
    for i in range(EARLY, 3):
        load(("mom", i), mom_hbm.at[blocks[i]], mom.at[blocks[i]])

    barrier = pltpu.get_barrier_semaphore()
    partners = [device[k] for k in ("y+", "y-", "z+", "z-", "far")] + peer_device
    for d in partners:
        pl.semaphore_signal(barrier, inc=1, device_id=d, device_id_type=MESH)
    own = pl.multiple_of(f * cols, BLOCK)

    def own_columns(t):
        first, width = TILES[t]
        return pl.ds(pl.multiple_of(own + first, BLOCK), width)

    def without_update():
        for i in range(EARLY):
            loads["base", i].wait()
            loads["mom", i].wait()
            for t, (first, width) in enumerate(TILES):
                span = pl.ds(first, width)
                z_ref[blocks[i], own_columns(t)] = (base[blocks[i], span] - OLD * mom[blocks[i], span]).astype(BF16)
        pl.semaphore_wait(barrier, len(partners))

    def positions(i):
        if i == 0:
            loads["keep"].wait()
        for t, (_, width) in enumerate(TILES):
            at_u, at_v = [], []
            for b in range(width // BLOCK):
                pos = keep[i, pl.ds(4 * t + b, 1), :]
                u = lax.broadcasted_iota(jnp.int32, (LOWF, 256), 0)
                v = lax.broadcasted_iota(jnp.int32, (4 * LOWF, 256), 0)
                at_u.append(jnp.where(u == pos // BLOCK, 1.0, 0.0).astype(BF16))
                at_v.append(jnp.where(v == pos % BLOCK + LOWF * b, 1.0, 0.0).astype(BF16))
            mask[pl.ds(LOWF * i, LOWF), pl.ds(BLOCK * t, BLOCK)] = lax.dot_general(
                jnp.concatenate(at_u, axis=1),
                jnp.concatenate(at_v, axis=1),
                (((1,), (1,)), ((), ())),
                preferred_element_type=F32,
            )

    def encode(i):
        if i == 0:
            loads["narrow"].wait()
        for name in ("base", "local", "err") if i >= EARLY else ("local", "err"):
            loads[name, i].wait()
        low = narrow[1024:1056], narrow[1056:1088]
        for t, (first, width) in enumerate(TILES):
            span = pl.ds(first, width)
            pseudo = base[blocks[i], span] - local[blocks[i], span] + err[blocks[i], span]
            e_ref[blocks[i], span] = pseudo
            half = three(halves(pseudo), (narrow[0:width], narrow[512 : 512 + width]))
            coef = three(low, halves(half))
            place = pl.ds(LOWF * i, LOWF), pl.ds(BLOCK * t, BLOCK)
            kept[place] = coef * mask[place]

    def travel(src, dst, n, device_id):
        copy = pltpu.make_async_remote_copy(
            src_ref=src, dst_ref=dst, send_sem=red_send.at[n], recv_sem=red_recv.at[n],
            device_id=device_id, device_id_type=MESH,
        )
        copy.start()
        return copy

    moving = {}

    def scatter():
        for t in range(4):
            for a in range(2):
                rs_send[4 * a + t] = kept[48 * a : 48 * a + 48, BLOCK * t : BLOCK * t + BLOCK].astype(BF16)
        moving["scatter"] = [travel(rs_send.at[peers[k]], rs_recv.at[k], k, peer_device[k]) for k in range(7)]

    def far():
        total = rs_send[group].astype(F32)
        for k in range(7):
            moving["scatter"][k].wait()
            total = total + rs_recv[k].astype(F32)
        part[0] = total.astype(BF16)
        moving["far"] = travel(part.at[0], part.at[1], 7, device["far"])

    def average():
        moving["far"].wait()
        mean[group] = ((part[0].astype(F32) + part[1].astype(F32)) * (1.0 / N_REPLICA)).astype(BF16)
        moving["mean"] = [travel(mean.at[group], mean.at[group], 8 + k, peer_device[k]) for k in range(7)]

    def averaged():
        for copy in moving["mean"]:
            copy.wait()
        for t in range(4):
            place = pl.ds(BLOCK * t, BLOCK)
            coef_ref[c, f, 0:16, place] = mean[t, pl.ds(pl.multiple_of(c * 32, 16), 16), :]
            coef_ref[c, f, 16:32, place] = mean[t + 4 * c, pl.ds(pl.multiple_of((1 - c) * 16, 16), 16), :]

    def residual(t):
        if t == 0:
            loads["wide"].wait()
        first, width = TILES[t]
        diag, span = diagonal(wide, width), pl.ds(first, width)
        high, rest = halves(kept[:, BLOCK * t : BLOCK * t + BLOCK])
        spread = columns_back(high, diag) + mm(rest, diag[:BLOCK])
        for i in range(3):
            back = rows_back(narrow[1088:1216, : 3 * LOWF], spread[LOWF * i : LOWF * i + LOWF])
            e_ref[blocks[i], span] = e_ref[blocks[i], span] - back

    def step(t):
        if t == 0:
            for i in range(EARLY, 3):
                loads["mom", i].wait()
        first, width = TILES[t]
        diag, span = diagonal(wide, width), pl.ds(first, width)
        spread = columns_back(jnp.concatenate([mean[t], mean[4 + t]], axis=0), diag)
        for i in range(3):
            update = rows_back(narrow[1088:1216, : 3 * LOWF], spread[LOWF * i : LOWF * i + LOWF])
            moved = outer_momentum * mom[blocks[i], span] + update
            m_ref[blocks[i], span] = moved
            if i >= EARLY:
                weights = base[blocks[i], span] - outer_rate * (update + outer_momentum * moved)
                z_ref[blocks[i], own_columns(t)] = weights.astype(BF16)

    nothing = lambda: None
    chain = [(("ready", 0), without_update, 2.6, 0)]
    chain += [(("mask", i), functools.partial(positions, i), 0.8, 0) for i in range(3)]
    chain += [(("encode", i), functools.partial(encode, i), 0.8, 0) for i in range(3)]
    chain += [("scatter", scatter, 0.9, 0)]
    chain += [(("residual", t), functools.partial(residual, t), 0.6, 1.5 * t) for t in (0, 1)]
    chain += [("far", far, 0.8, 0)]
    chain += [(("residual", t), functools.partial(residual, t), 0.6, 3.0 * (t - 2)) for t in (2, 3)]
    chain += [("average", average, 0.9, 2.5), (("ready", "k"), averaged, 0.5, 0)]
    chain += [(("update", t), functools.partial(step, t), 0.7, 0) for t in range(4)]
    chain += [(("ready", 1), nothing, 0, 0), (("ready", 2), nothing, 0, 0)]
    compute = {name: run for name, run, _, _ in chain}

    arrivals, departures, sent, received = {}, {}, {}, {}

    def index(table, key):
        return table.setdefault(key, len(table))

    def copy(unit, way, recv_key):
        s, p, a, b, h = unit
        if p == "k":
            if a == "all":
                ref, rows, width = coef_ref.at[c], 16, 16
            else:
                dy, dz = a + c * (b - a), b + c * (a - b)
                shard = ((y + dy) % 4) * 4 + (zl + dz) % 4
                ref, rows, width = coef_ref.at[c, shard], 16, 1
            target = device["pair"] if way == "pair" else device["k", way]
        else:
            start, count, outer, middle = STAGES[s]
            top = start + c * count
            size = {"m": middle, "o": outer, "q": outer, "mo": outer + middle, "all": count}
            row = {
                "m": top + outer, "o": top + odd * (outer + middle),
                "q": top + (1 - odd) * (outer + middle), "mo": top + odd * outer, "all": top,
            }
            dy, dz = (a, b) if p in ("m", "mo", "all") else (b, a)
            column = (((y + dy) % 4) * 4 + (zl + dz) % 4) * cols + (h or 0) * (cols // 2)
            rows, width = size[p], cols if h is None else cols // 2
            ref = z_ref.at[pl.ds(pl.multiple_of(row[p], 16), rows), pl.ds(pl.multiple_of(column, BLOCK), width)]
            axes = {"A": "yz"[p == "o"], "B": "zy"[p == "o"]}
            target = device[axes[way[0]] + way[1] if way[0] in "AB" else way]
        out = s, p, way
        made = pltpu.make_async_remote_copy(
            src_ref=ref, dst_ref=ref, send_sem=out_sem.at[index(departures, out)],
            recv_sem=in_sem.at[index(arrivals, recv_key)], device_id=target, device_id_type=MESH,
        )
        return made, out, rows, width

    def send(unit, way):
        s, p, a, b, h = unit
        key = (s, p, "pair") if way == "pair" else (s,) + lands(p, a, b, way) + (h,)
        made, out, rows, width = copy(unit, way, key)
        sent[out] = (rows, sent.get(out, (rows, 0))[1] + width)
        if way == "pair":
            received[key] = sent[out]
        made.start()

    def arrive(unit):
        copy(unit, "pair", unit)[0].wait_recv()

    for name, waits, sends in order(STAGES, [(n, cost, gap) for n, _, cost, gap in chain]):
        for unit in waits:
            arrive(unit)
        if name in compute:
            compute[name]()
        for unit, way in sends:
            send(unit, way)

    def drain(p, rows, width, out_key, in_key):
        if p == "k":
            ref = coef_ref.at[0, pl.ds(0, width)]
        else:
            ref = z_ref.at[pl.ds(0, rows), pl.ds(0, width)]
        return pltpu.make_async_remote_copy(
            src_ref=ref, dst_ref=ref, send_sem=out_sem.at[departures[out_key]],
            recv_sem=in_sem.at[arrivals[in_key]], device_id=device["pair"], device_id_type=MESH,
        )

    some = next(iter(received))
    for out, (rows, width) in sent.items():
        drain(out[1], rows, width, out, some).wait_send()
    for key, (rows, width) in received.items():
        drain(key[1], rows, width, key, key).wait_recv()


def store(
    z_ref, e_ref, m_ref, coef_ref, wide_hbm, narrow_hbm, w_out, e_out, m_out,
    wide, turned, spread, slots, sem, slot_sem,
):
    cols = e_ref.shape[1]
    tables = [
        pltpu.make_async_copy(wide_hbm, wide, sem.at[3, 0]),
        pltpu.make_async_copy(narrow_hbm.at[pl.ds(1216, BLOCK)], turned, sem.at[3, 1]),
    ]
    shards = coef_ref.shape[1]
    n = slots.shape[0]
    turns = shards // n

    def rest(k):
        pieces = []
        for m, (src, dst, first) in enumerate(((z_ref, w_out, EARLY * BLOCK), (e_ref, e_out.at[0], 0), (m_ref, m_out, 0))):
            height = (src.shape[0] - first) // turns
            lines = pl.ds(pl.multiple_of(first + height * k, 16), height)
            pieces.append(pltpu.make_async_copy(src.at[lines], dst.at[lines], sem.at[m, k]))
        return pieces

    for copy in tables:
        copy.start()
    ahead = turns // 2
    for k in range(ahead):
        for copy in rest(k):
            copy.start()
    for copy in tables:
        copy.wait()

    def out(slot, shard, i):
        block = pl.ds(BLOCK * i, BLOCK)
        span = pl.ds(pl.multiple_of(shard * cols, BLOCK), cols)
        return pltpu.make_async_copy(slots.at[slot, block], w_out.at[block, span], slot_sem.at[slot, i])

    for i in range(EARLY):
        for t, (first, width) in enumerate(TILES):
            coef = coef_ref[i, :, :, pl.ds(BLOCK * t, BLOCK)].reshape(shards * LOWF, BLOCK)
            spread[i, :, pl.ds(first, width)] = columns_back(coef, diagonal(wide, width)).astype(BF16)

    table = turned[:, : 2 * LOWF]

    def place(slot, shard, again):
        lines = pl.ds(pl.multiple_of(shard * LOWF, LOWF), LOWF)
        for i in range(EARLY):
            pl.when(again)(lambda i=i: out(slot, shard, i).wait())
            block = pl.ds(BLOCK * i, BLOCK)
            for first, width in ((0, cols // 2), (cols // 2, cols // 2)):
                span = pl.ds(first, width)
                one = spread[i, lines, span]
                update = mm(table, jnp.concatenate([one, one], axis=0))
                before = z_ref[block, pl.ds(pl.multiple_of(shard * cols + first, BLOCK), width)].astype(F32)
                slots[slot, block, span] = (before + update).astype(BF16)
            out(slot, shard, i).start()

    def turn(k, carry):
        for slot in range(n):
            place(slot, k * n + slot, k > 0)

        @pl.when(k + ahead < turns)
        def _():
            for copy in rest(k + ahead):
                copy.start()

        return carry

    lax.fori_loop(0, turns, turn, 0)
    for slot in range(n):
        for i in range(EARLY):
            out(slot, shards - n + slot, i).wait()
    for k in range(turns):
        for copy in rest(k):
            copy.wait()


def body(local_weights, base_weights, error_buffer, momentum, keep_index):
    rows, cols = base_weights.shape
    shards = lax.axis_size("fsdp")
    wide, narrow = (jnp.asarray(table) for table in tables())
    hbm = pl.BlockSpec(memory_space=pltpu.HBM)
    vmem = pl.BlockSpec(memory_space=pltpu.VMEM)
    z, e, m, coef = pl.pallas_call(
        kernel,
        out_shape=(
            pltpu.VMEM((rows, shards * cols), BF16),
            pltpu.VMEM((rows, cols), F32),
            pltpu.VMEM((rows, cols), F32),
            pltpu.VMEM((EARLY, shards, LOWF, 512), BF16),
        ),
        in_specs=[hbm] * 7,
        out_specs=[vmem] * 4,
        scratch_shapes=[pltpu.VMEM((rows, cols), F32)] * 4
        + [
            pltpu.VMEM((3, 14, 256), jnp.int32),
            pltpu.VMEM((1024, 128), BF16),
            pltpu.VMEM((1344, 128), BF16),
            pltpu.VMEM((96, 512), F32),
            pltpu.VMEM((96, 512), F32),
            pltpu.VMEM((8, 48, 128), BF16),
            pltpu.VMEM((7, 48, 128), BF16),
            pltpu.VMEM((2, 48, 128), BF16),
            pltpu.VMEM((8, 48, 128), BF16),
            pltpu.SemaphoreType.DMA((15,)),
            pltpu.SemaphoreType.DMA((15,)),
            pltpu.SemaphoreType.DMA((15,)),
            pltpu.SemaphoreType.DMA((64,)),
            pltpu.SemaphoreType.DMA((256,)),
        ],
        compiler_params=pltpu.CompilerParams(
            collective_id=1, has_side_effects=True, vmem_limit_bytes=35 << 20
        ),
        name="step",
    )(
        local_weights,
        base_weights,
        error_buffer,
        momentum,
        keep_index.transpose(1, 0, 2),
        wide,
        narrow,
    )
    weights, new_error, new_momentum = pl.pallas_call(
        store,
        out_shape=(
            jax.ShapeDtypeStruct((rows, shards * cols), BF16),
            jax.ShapeDtypeStruct((1, rows, cols), F32),
            jax.ShapeDtypeStruct((rows, cols), F32),
        ),
        in_specs=[vmem] * 4 + [hbm] * 2,
        out_specs=[pl.BlockSpec(memory_space=pl.ANY)] * 3,
        scratch_shapes=[
            pltpu.VMEM((1024, 128), BF16),
            pltpu.VMEM((128, 128), BF16),
            pltpu.VMEM((EARLY, shards * LOWF, cols), BF16),
            pltpu.VMEM((2, EARLY * BLOCK, cols), BF16),
            pltpu.SemaphoreType.DMA((4, 8)),
            pltpu.SemaphoreType.DMA((2, EARLY)),
        ],
        compiler_params=pltpu.CompilerParams(vmem_limit_bytes=6 << 20),
        name="store",
    )(z, e, m, coef, wide, narrow)
    return new_momentum, new_error, weights


def solution(mesh):
    return jax.shard_map(
        body,
        mesh=mesh,
        in_specs=(
            P("replica", None, "fsdp"),
            P(None, "fsdp"),
            P("replica", None, "fsdp"),
            P(None, "fsdp"),
            P("fsdp", None, None),
        ),
        out_specs=(P(None, "fsdp"), P("replica", None, "fsdp"), P()),
        check_vma=False,
    )
```

```python
import functools

import jax
import jax.numpy as jnp
import ml_dtypes
import numpy as np
from jax import lax
from jax.experimental import pallas as pl
from jax.experimental.pallas import tpu as pltpu
from jax.sharding import PartitionSpec as P

MESH = pl.DeviceIdType.MESH
BLOCK = 128
LOWF = 32
N_REPLICA = 16
F32 = jnp.float32
BF16 = jnp.bfloat16
outer_rate = 0.7
outer_momentum = 0.9
OLD = outer_rate * outer_momentum * outer_momentum
NEW = outer_rate * (1.0 + outer_momentum)

TILES = ((0, 512), (512, 512), (1024, 512), (1536, 256))
STAGES = ((0, 128, 48, 32), (256, 48, 16, 16), (352, 16, 0, 16))
EARLY = 2

WAYS = ("y+", "y-", "z+", "z-", "x+", "x-", "pair")
PLACES = [(a, b) for a in (0, 1, 3, 2) for b in (0, 1, 3, 2)][1:]


def lands(part, a, b, way):
    if way in ("x+", "x-"):
        return "q", a, b
    step = -1 if way[1] == "+" else 1
    if way[0] == "A":
        return part, (a + step) % 4, b
    return part, a, (b + step) % 4


def tasks(stages, k_stage=True, pair="split"):
    todo = []

    def add(name, waits, sends, after=()):
        todo.append((name, tuple(waits), tuple(sends), tuple(after)))

    for s, (_, _, outer, middle) in enumerate(stages):
        parts = [p for p, n in (("m", middle), ("o", outer)) if n]

        def u(p, a, b, h=None):
            return s, p, a % 4, b % 4, h

        own = [(u(p, 0, 0), w + sign) for w in "AB" for p in parts for sign in "+-"]
        add(("own", s), [], own, [("ready", s)])
        for p in parts:

            def x(a, b, way, h=None):
                return [(u(p, a, b, h), way)] if p == "o" else []

            for a, sign, h in ((3, "+", 0), (1, "-", 1)):
                sends = [(u(p, a, 0, h), "A" + sign), (u(p, a, 0), "B+"), (u(p, a, 0), "B-")]
                add(("A", s, p, a), [u(p, a, 0)], sends + x(a, 0, "x" + sign))
                add(("H", s, p, h), [u(p, 2, 0, h)], x(2, 0, "x" + sign, h))
            add(("D", s, p), [], [(u(p, 2, 0), "B+"), (u(p, 2, 0), "B-")], [("H", s, p, 0), ("H", s, p, 1)])
            for a in range(4):
                for b, sign in ((3, "+"), (1, "-")):
                    on = [(u(p, a, b), "B" + sign)] if sign == ("+" if a in (0, 1) else "-") else []
                    add(("B", s, p, a, b), [u(p, a, b)], on + x(a, b, "x" + sign))
                add(("B", s, p, a, 2), [u(p, a, 2)], x(a, 2, "x+" if a in (0, 1) else "x-"))
        for dy, dz in PLACES:
            done = []
            for p in parts:
                a, b = (dy, dz) if p == "m" else (dz, dy)
                done.append(("D", s, p) if (a, b) == (2, 0) else ("A", s, p, a) if b == 0 else ("B", s, p, a, b))
            hs = (0, 1) if (dz, dy) == (2, 0) else (None,)
            waits = [u("q", dz, dy, h) for h in hs] if outer else []
            if pair == "all" or not outer:
                add(("P", s, dy, dz), waits, [(u("all", dy, dz), "pair")], done)
            else:
                add(("PM", s, dy, dz), [], [(u("mo", dy, dz), "pair")], done)
                add(("PQ", s, dy, dz), waits, [(u("q", dz, dy), "pair")])
    if k_stage:
        def u(a, b):
            return 0, "k", a % 4, b % 4, None

        add(("own", "k"), [], [(u(0, 0), w + sign) for w in "AB" for sign in "+-"], [("ready", "k")])
        names = []
        for a, sends in ((3, [(u(3, 0), "A+")]), (1, []), (2, [])):
            add(("A", "k", a), [u(a, 0)], sends + [(u(a, 0), "B+"), (u(a, 0), "B-")])
            names.append(("A", "k", a))
        for a in range(4):
            for b, sign in ((3, "+"), (1, "-")):
                on = [(u(a, b), "B" + sign)] if sign == ("+" if a in (0, 1) else "-") else []
                add(("B", "k", a, b), [u(a, b)], on)
            add(("B", "k", a, 2), [u(a, 2)], [])
            names += [("B", "k", a, b) for b in (1, 2, 3)]
        add(("P", "k"), [], [((0, "k", "all", 0, None), "pair")], names)
    return todo


def rows_of(stages, unit):
    s, p, _, _, h = unit
    _, count, outer, middle = stages[s]
    n = {"m": middle, "o": outer, "q": outer, "all": count, "mo": outer + middle, "k": LOWF * 512 / 1792}[p]
    if p == "k" and unit[2] == "all":
        n *= 16
    return n * (1 if h is None else 0.5)


def order(stages, chain, k_stage=True, pair="split", cs=0.12, cw=0.06, lat=3.0, rate=45.5e3, prate=500e3, t0=0.0):
    todo = tasks(stages, k_stage, pair)
    for n, (name, cost, gap) in enumerate(chain):
        todo.append((name, (), (), (chain[n - 1][0],) if n else ()))
    cost = {name: (c, gap) for name, c, gap in chain}
    rank = {"own": 0, "A": 1, "H": 1, "D": 1, "B": 2, "PM": 4, "PQ": 4, "P": 4}
    arrival, free, done, t, out, left = {}, {}, {}, t0, [], list(todo)
    while left:
        best = None
        for n, (name, waits, sends, after) in enumerate(left):
            if any(k not in done for k in after) or any(k not in arrival for k in waits):
                continue
            ready = max([done[k] for k in after] + [arrival[k] for k in waits] + [0])
            r = 3 if name in cost else rank[name[0]]
            if r == 2 and not sends: r = 4
            key = (max(ready, t), r, ready, n)
            if best is None or key < best[0]:
                best = (key, n)
        key, n = best
        name, waits, sends, after = left.pop(n)
        t = max(t, key[0])
        gap = 0
        if name in cost:
            t += cost[name][0]
            gap = cost[name][1]
        t += cw * len(waits)
        for unit, way in sends:
            t += cs
            s, p, a, b, h = unit
            lane = way
            if way[0] in "AB":
                first = p in ("m", "k")
                lane = ("y" if (way[0] == "A") == first else "z") + way[1]
            size = rows_of(stages, unit) * 1792 * 2
            start = max(t, free.get(lane, 0))
            free[lane] = start + size / (prate if way == "pair" else rate)
            if way == "pair":
                arrival["pair", s] = max(arrival.get(("pair", s), 0), free[lane] + lat)
            else:
                q, a2, b2 = lands(p, a, b, way)
                arrival[s, q, a2, b2, h] = free[lane] + lat
        done[name] = t + gap
        out.append((name, waits, sends))
    return out


def split(values):
    high = values.astype(ml_dtypes.bfloat16)
    low = (values - high.astype(np.float64)).astype(ml_dtypes.bfloat16)
    return high, low


def tables():
    u = np.arange(LOWF, dtype=np.float64)[:, None]
    a = np.arange(BLOCK, dtype=np.float64)[None, :]
    norm = np.where(u == 0, np.sqrt(1.0 / BLOCK), np.sqrt(2.0 / BLOCK))
    low = norm * np.cos(np.pi * (2 * a + 1) * u / (2 * BLOCK))
    step = split(-NEW * low.T)
    diag = np.kron(np.eye(4), low)
    wide = np.concatenate(split(diag), axis=0)
    wide = np.concatenate([wide[:, BLOCK * n : BLOCK * n + BLOCK] for n in range(4)], axis=0)
    high, rest = split(low.T)
    turned = np.concatenate([high, rest, high, np.zeros_like(high)], axis=1)
    step = np.concatenate(step + (np.zeros((BLOCK, 2 * LOWF), ml_dtypes.bfloat16),), axis=1)
    narrow = np.concatenate(split(diag.T) + split(low) + (turned, step), axis=0)
    return wide, narrow


def mm(a, b):
    return jnp.dot(a, b, preferred_element_type=F32)


def halves(v):
    high = v.astype(BF16)
    return high, (v - high.astype(F32)).astype(BF16)


def three(a, b):
    return mm(a[0], b[0]) + (mm(a[1], b[0]) + mm(a[0], b[1]))


def diagonal(wide, width):
    return jnp.concatenate([wide[256 * n : 256 * n + 256] for n in range(width // BLOCK)], axis=1)


def columns_back(coef, diag):
    return mm(jnp.concatenate([coef, coef], axis=1), diag)


def rows_back(turned, spread):
    high, rest = halves(spread)
    return mm(turned, jnp.concatenate([high, high, rest], axis=0))


def kernel(
    local_hbm, base_hbm, err_hbm, mom_hbm, keep_hbm, wide_hbm, narrow_hbm,
    z_ref, e_ref, m_ref, coef_ref,
    local, base, err, mom, keep, wide, narrow,
    mask, kept, rs_send, rs_recv, part, mean,
    load_sem, red_send, red_recv, out_sem, in_sem,
):
    r, f = lax.axis_index("replica"), lax.axis_index("fsdp")
    x, zh, c = r // 4, (r // 2) % 2, r % 2
    y, zl = f // 4, f % 4
    z = zh * 4 + zl
    cols = e_ref.shape[1]
    group = x * 2 + c
    odd = x % 2

    def at(x_, y_, z_, c_):
        return ((x_ * 2 + z_ // 4) * 2 + c_, y_ * 4 + z_ % 4)

    device = {
        "x+": at((x + 1) % 4, y, z, c), "x-": at((x + 3) % 4, y, z, c),
        "y+": at(x, (y + 1) % 4, z, c), "y-": at(x, (y + 3) % 4, z, c),
        "z+": at(x, y, (z + 1) % 8, c), "z-": at(x, y, (z + 7) % 8, c),
        "far": at(x, y, (z + 4) % 8, c), "pair": at(x, y, z, 1 - c),
    }
    for sign in "+-":
        one, two = device["y" + sign], device["z" + sign]
        device["k", "A" + sign] = tuple(p * (1 - c) + q * c for p, q in zip(one, two, strict=True))
        device["k", "B" + sign] = tuple(p * c + q * (1 - c) for p, q in zip(one, two, strict=True))
    peers = [(group + k) % 8 for k in range(1, 8)]
    peer_device = [at(p // 2, y, z, p % 2) for p in peers]

    loads = {}

    def load(name, src, dst):
        loads[name] = pltpu.make_async_copy(src, dst, load_sem.at[len(loads)])
        loads[name].start()

    blocks = [pl.ds(BLOCK * i, BLOCK) for i in range(3)]
    for i in range(EARLY):
        load(("base", i), base_hbm.at[blocks[i]], base.at[blocks[i]])
        load(("mom", i), mom_hbm.at[blocks[i]], mom.at[blocks[i]])
    load("keep", keep_hbm, keep)
    load("narrow", narrow_hbm, narrow)
    for i in range(3):
        load(("local", i), local_hbm.at[0, blocks[i]], local.at[blocks[i]])
        load(("err", i), err_hbm.at[0, blocks[i]], err.at[blocks[i]])
        if i >= EARLY:
            load(("base", i), base_hbm.at[blocks[i]], base.at[blocks[i]])
    load("wide", wide_hbm, wide)
    for i in range(EARLY, 3):
        load(("mom", i), mom_hbm.at[blocks[i]], mom.at[blocks[i]])

    barrier = pltpu.get_barrier_semaphore()
    partners = [device[k] for k in ("y+", "y-", "z+", "z-", "far")] + peer_device
    for d in partners:
        pl.semaphore_signal(barrier, inc=1, device_id=d, device_id_type=MESH)
    own = pl.multiple_of(f * cols, BLOCK)

    def own_columns(t):
        first, width = TILES[t]
        return pl.ds(pl.multiple_of(own + first, BLOCK), width)

    def without_update():
        for i in range(EARLY):
            loads["base", i].wait()
            loads["mom", i].wait()
            for t, (first, width) in enumerate(TILES):
                span = pl.ds(first, width)
                z_ref[blocks[i], own_columns(t)] = (base[blocks[i], span] - OLD * mom[blocks[i], span]).astype(BF16)
        pl.semaphore_wait(barrier, len(partners))

    def positions(i):
        if i == 0:
            loads["keep"].wait()
        for t, (_, width) in enumerate(TILES):
            at_u, at_v = [], []
            for b in range(width // BLOCK):
                pos = keep[i, pl.ds(4 * t + b, 1), :]
                u = lax.broadcasted_iota(jnp.int32, (LOWF, 256), 0)
                v = lax.broadcasted_iota(jnp.int32, (4 * LOWF, 256), 0)
                at_u.append(jnp.where(u == pos // BLOCK, 1.0, 0.0).astype(BF16))
                at_v.append(jnp.where(v == pos % BLOCK + LOWF * b, 1.0, 0.0).astype(BF16))
            mask[pl.ds(LOWF * i, LOWF), pl.ds(BLOCK * t, BLOCK)] = lax.dot_general(
                jnp.concatenate(at_u, axis=1),
                jnp.concatenate(at_v, axis=1),
                (((1,), (1,)), ((), ())),
                preferred_element_type=F32,
            )

    def encode(i):
        if i == 0:
            loads["narrow"].wait()
        for name in ("base", "local", "err") if i >= EARLY else ("local", "err"):
            loads[name, i].wait()
        low = narrow[1024:1056], narrow[1056:1088]
        for t, (first, width) in enumerate(TILES):
            span = pl.ds(first, width)
            pseudo = base[blocks[i], span] - local[blocks[i], span] + err[blocks[i], span]
            e_ref[blocks[i], span] = pseudo
            half = three(halves(pseudo), (narrow[0:width], narrow[512 : 512 + width]))
            coef = three(low, halves(half))
            place = pl.ds(LOWF * i, LOWF), pl.ds(BLOCK * t, BLOCK)
            kept[place] = coef * mask[place]

    def travel(src, dst, n, device_id):
        copy = pltpu.make_async_remote_copy(
            src_ref=src, dst_ref=dst, send_sem=red_send.at[n], recv_sem=red_recv.at[n],
            device_id=device_id, device_id_type=MESH,
        )
        copy.start()
        return copy

    moving = {}

    def scatter():
        for t in range(4):
            for a in range(2):
                rs_send[4 * a + t] = kept[48 * a : 48 * a + 48, BLOCK * t : BLOCK * t + BLOCK].astype(BF16)
        moving["scatter"] = [travel(rs_send.at[peers[k]], rs_recv.at[k], k, peer_device[k]) for k in range(7)]

    def far():
        total = rs_send[group].astype(F32)
        for k in range(7):
            moving["scatter"][k].wait()
            total = total + rs_recv[k].astype(F32)
        part[0] = total.astype(BF16)
        moving["far"] = travel(part.at[0], part.at[1], 7, device["far"])

    def average():
        moving["far"].wait()
        mean[group] = ((part[0].astype(F32) + part[1].astype(F32)) * (1.0 / N_REPLICA)).astype(BF16)
        moving["mean"] = [travel(mean.at[group], mean.at[group], 8 + k, peer_device[k]) for k in range(7)]

    def averaged():
        for copy in moving["mean"]:
            copy.wait()
        for t in range(4):
            place = pl.ds(BLOCK * t, BLOCK)
            coef_ref[c, f, 0:16, place] = mean[t, pl.ds(pl.multiple_of(c * 32, 16), 16), :]
            coef_ref[c, f, 16:32, place] = mean[t + 4 * c, pl.ds(pl.multiple_of((1 - c) * 16, 16), 16), :]

    def residual(t):
        if t == 0:
            loads["wide"].wait()
        first, width = TILES[t]
        diag, span = diagonal(wide, width), pl.ds(first, width)
        high, rest = halves(kept[:, BLOCK * t : BLOCK * t + BLOCK])
        spread = columns_back(high, diag) + mm(rest, diag[:BLOCK])
        for i in range(3):
            back = rows_back(narrow[1088:1216, : 3 * LOWF], spread[LOWF * i : LOWF * i + LOWF])
            e_ref[blocks[i], span] = e_ref[blocks[i], span] - back

    def step(t):
        if t == 0:
            for i in range(EARLY, 3):
                loads["mom", i].wait()
        first, width = TILES[t]
        diag, span = diagonal(wide, width), pl.ds(first, width)
        spread = columns_back(jnp.concatenate([mean[t], mean[4 + t]], axis=0), diag)
        for i in range(3):
            update = rows_back(narrow[1088:1216, : 3 * LOWF], spread[LOWF * i : LOWF * i + LOWF])
            moved = outer_momentum * mom[blocks[i], span] + update
            m_ref[blocks[i], span] = moved
            if i >= EARLY:
                weights = base[blocks[i], span] - outer_rate * (update + outer_momentum * moved)
                z_ref[blocks[i], own_columns(t)] = weights.astype(BF16)

    nothing = lambda: None
    chain = [(("ready", 0), without_update, 2.6, 0)]
    chain += [(("mask", i), functools.partial(positions, i), 0.8, 0) for i in range(3)]
    chain += [(("encode", i), functools.partial(encode, i), 0.8, 0) for i in range(3)]
    chain += [("scatter", scatter, 0.9, 0)]
    chain += [(("residual", t), functools.partial(residual, t), 0.6, 1.5 * t) for t in (0, 1)]
    chain += [("far", far, 0.8, 0)]
    chain += [(("residual", t), functools.partial(residual, t), 0.6, 3.0 * (t - 2)) for t in (2, 3)]
    chain += [("average", average, 0.9, 2.5), (("ready", "k"), averaged, 0.5, 0)]
    chain += [(("update", t), functools.partial(step, t), 0.7, 0) for t in range(4)]
    chain += [(("ready", 1), nothing, 0, 0), (("ready", 2), nothing, 0, 0)]
    compute = {name: run for name, run, _, _ in chain}

    arrivals, departures, sent, received = {}, {}, {}, {}

    def index(table, key):
        return table.setdefault(key, len(table))

    def copy(unit, way, recv_key):
        s, p, a, b, h = unit
        if p == "k":
            if a == "all":
                ref, rows, width = coef_ref.at[c], 16, 16
            else:
                dy, dz = a + c * (b - a), b + c * (a - b)
                shard = ((y + dy) % 4) * 4 + (zl + dz) % 4
                ref, rows, width = coef_ref.at[c, shard], 16, 1
            target = device["pair"] if way == "pair" else device["k", way]
        else:
            start, count, outer, middle = STAGES[s]
            top = start + c * count
            size = {"m": middle, "o": outer, "q": outer, "mo": outer + middle, "all": count}
            row = {
                "m": top + outer, "o": top + odd * (outer + middle),
                "q": top + (1 - odd) * (outer + middle), "mo": top + odd * outer, "all": top,
            }
            dy, dz = (a, b) if p in ("m", "mo", "all") else (b, a)
            column = (((y + dy) % 4) * 4 + (zl + dz) % 4) * cols + (h or 0) * (cols // 2)
            rows, width = size[p], cols if h is None else cols // 2
            ref = z_ref.at[pl.ds(pl.multiple_of(row[p], 16), rows), pl.ds(pl.multiple_of(column, BLOCK), width)]
            axes = {"A": "yz"[p == "o"], "B": "zy"[p == "o"]}
            target = device[axes[way[0]] + way[1] if way[0] in "AB" else way]
        out = s, p, way
        made = pltpu.make_async_remote_copy(
            src_ref=ref, dst_ref=ref, send_sem=out_sem.at[index(departures, out)],
            recv_sem=in_sem.at[index(arrivals, recv_key)], device_id=target, device_id_type=MESH,
        )
        return made, out, rows, width

    def send(unit, way):
        s, p, a, b, h = unit
        key = (s, p, "pair") if way == "pair" else (s,) + lands(p, a, b, way) + (h,)
        made, out, rows, width = copy(unit, way, key)
        sent[out] = (rows, sent.get(out, (rows, 0))[1] + width)
        if way == "pair":
            received[key] = sent[out]
        made.start()

    def arrive(unit):
        copy(unit, "pair", unit)[0].wait_recv()

    for name, waits, sends in order(STAGES, [(n, cost, gap) for n, _, cost, gap in chain]):
        for unit in waits:
            arrive(unit)
        if name in compute:
            compute[name]()
        for unit, way in sends:
            send(unit, way)

    def drain(p, rows, width, out_key, in_key):
        if p == "k":
            ref = coef_ref.at[0, pl.ds(0, width)]
        else:
            ref = z_ref.at[pl.ds(0, rows), pl.ds(0, width)]
        return pltpu.make_async_remote_copy(
            src_ref=ref, dst_ref=ref, send_sem=out_sem.at[departures[out_key]],
            recv_sem=in_sem.at[arrivals[in_key]], device_id=device["pair"], device_id_type=MESH,
        )

    some = next(iter(received))
    for out, (rows, width) in sent.items():
        drain(out[1], rows, width, out, some).wait_send()
    for key, (rows, width) in received.items():
        drain(key[1], rows, width, key, key).wait_recv()


def store(
    z_ref, e_ref, m_ref, coef_ref, wide_hbm, narrow_hbm, w_out, e_out, m_out,
    wide, turned, spread, slots, sem, slot_sem,
):
    cols = e_ref.shape[1]
    tables = [
        pltpu.make_async_copy(wide_hbm, wide, sem.at[3, 0]),
        pltpu.make_async_copy(narrow_hbm.at[pl.ds(1216, BLOCK)], turned, sem.at[3, 1]),
    ]
    shards = coef_ref.shape[1]
    n = slots.shape[0]
    turns = shards // n

    def rest(k):
        pieces = []
        for m, (src, dst, first) in enumerate(((z_ref, w_out, EARLY * BLOCK), (e_ref, e_out.at[0], 0), (m_ref, m_out, 0))):
            height = (src.shape[0] - first) // turns
            lines = pl.ds(pl.multiple_of(first + height * k, 16), height)
            pieces.append(pltpu.make_async_copy(src.at[lines], dst.at[lines], sem.at[m, k]))
        return pieces

    for copy in tables:
        copy.start()
    ahead = turns // 2
    for k in range(ahead):
        for copy in rest(k):
            copy.start()
    for copy in tables:
        copy.wait()

    def out(slot, shard, i):
        block = pl.ds(BLOCK * i, BLOCK)
        span = pl.ds(pl.multiple_of(shard * cols, BLOCK), cols)
        return pltpu.make_async_copy(slots.at[slot, block], w_out.at[block, span], slot_sem.at[slot, i])

    for i in range(EARLY):
        for t, (first, width) in enumerate(TILES):
            coef = coef_ref[i, :, :, pl.ds(BLOCK * t, BLOCK)].reshape(shards * LOWF, BLOCK)
            spread[i, :, pl.ds(first, width)] = columns_back(coef, diagonal(wide, width)).astype(BF16)

    table = turned[:, : 2 * LOWF]

    def place(slot, shard, again):
        lines = pl.ds(pl.multiple_of(shard * LOWF, LOWF), LOWF)
        for i in range(EARLY):
            pl.when(again)(lambda i=i: out(slot, shard, i).wait())
            block = pl.ds(BLOCK * i, BLOCK)
            for first, width in ((0, cols // 2), (cols // 2, cols // 2)):
                span = pl.ds(first, width)
                one = spread[i, lines, span]
                update = mm(table, jnp.concatenate([one, one], axis=0))
                before = z_ref[block, pl.ds(pl.multiple_of(shard * cols + first, BLOCK), width)].astype(F32)
                slots[slot, block, span] = (before + update).astype(BF16)
            out(slot, shard, i).start()

    def turn(k, carry):
        for slot in range(n):
            place(slot, k * n + slot, k > 0)

        @pl.when(k + ahead < turns)
        def _():
            for copy in rest(k + ahead):
                copy.start()

        return carry

    lax.fori_loop(0, turns, turn, 0)
    for slot in range(n):
        for i in range(EARLY):
            out(slot, shards - n + slot, i).wait()
    for k in range(turns):
        for copy in rest(k):
            copy.wait()


def body(local_weights, base_weights, error_buffer, momentum, keep_index):
    rows, cols = base_weights.shape
    shards = lax.axis_size("fsdp")
    wide, narrow = (jnp.asarray(table) for table in tables())
    hbm = pl.BlockSpec(memory_space=pltpu.HBM)
    vmem = pl.BlockSpec(memory_space=pltpu.VMEM)
    z, e, m, coef = pl.pallas_call(
        kernel,
        out_shape=(
            pltpu.VMEM((rows, shards * cols), BF16),
            pltpu.VMEM((rows, cols), F32),
            pltpu.VMEM((rows, cols), F32),
            pltpu.VMEM((EARLY, shards, LOWF, 512), BF16),
        ),
        in_specs=[hbm] * 7,
        out_specs=[vmem] * 4,
        scratch_shapes=[pltpu.VMEM((rows, cols), F32)] * 4
        + [
            pltpu.VMEM((3, 14, 256), jnp.int32),
            pltpu.VMEM((1024, 128), BF16),
            pltpu.VMEM((1344, 128), BF16),
            pltpu.VMEM((96, 512), F32),
            pltpu.VMEM((96, 512), F32),
            pltpu.VMEM((8, 48, 128), BF16),
            pltpu.VMEM((7, 48, 128), BF16),
            pltpu.VMEM((2, 48, 128), BF16),
            pltpu.VMEM((8, 48, 128), BF16),
            pltpu.SemaphoreType.DMA((15,)),
            pltpu.SemaphoreType.DMA((15,)),
            pltpu.SemaphoreType.DMA((15,)),
            pltpu.SemaphoreType.DMA((64,)),
            pltpu.SemaphoreType.DMA((256,)),
        ],
        compiler_params=pltpu.CompilerParams(
            collective_id=1, has_side_effects=True, vmem_limit_bytes=35 << 20
        ),
        name="step",
    )(
        local_weights,
        base_weights,
        error_buffer,
        momentum,
        keep_index.transpose(1, 0, 2),
        wide,
        narrow,
    )
    weights, new_error, new_momentum = pl.pallas_call(
        store,
        out_shape=(
            jax.ShapeDtypeStruct((rows, shards * cols), BF16),
            jax.ShapeDtypeStruct((1, rows, cols), F32),
            jax.ShapeDtypeStruct((rows, cols), F32),
        ),
        in_specs=[vmem] * 4 + [hbm] * 2,
        out_specs=[pl.BlockSpec(memory_space=pl.ANY)] * 3,
        scratch_shapes=[
            pltpu.VMEM((1024, 128), BF16),
            pltpu.VMEM((128, 128), BF16),
            pltpu.VMEM((EARLY, shards * LOWF, cols), BF16),
            pltpu.VMEM((2, EARLY * BLOCK, cols), BF16),
            pltpu.SemaphoreType.DMA((4, 8)),
            pltpu.SemaphoreType.DMA((2, EARLY)),
        ],
        compiler_params=pltpu.CompilerParams(vmem_limit_bytes=6 << 20),
        name="store",
    )(z, e, m, coef, wide, narrow)
    return new_momentum, new_error, weights


def solution(mesh):
    return jax.shard_map(
        body,
        mesh=mesh,
        in_specs=(
            P("replica", None, "fsdp"),
            P(None, "fsdp"),
            P("replica", None, "fsdp"),
            P(None, "fsdp"),
            P("fsdp", None, None),
        ),
        out_specs=(P(None, "fsdp"), P("replica", None, "fsdp"), P()),
        check_vma=False,
    )
```
